512 devices in a mesh: rows: 16 (over y, z_hi), lat: 32 (over x, z_lo, core).
Axes of the slice: x: 4, y: 4, z: 16 (z_hi: 4, z_lo: 4; z = z_hi * 4 + z_lo), core: 2. Of those that a mesh axis runs over, the one named last changes fastest.
Arguments:
- activations: bfloat16 [65536, 3584], P(('rows', 'lat')), may hold values from -6 to 6
- block_ids: int32 [65536, 2], P(('rows', 'lat')), may hold values from 0 to 31, all different within a row; in each aligned block of 128 rows (0 to 127, 128 to 255, ...) at most 12 rows name the same one
- enc_weight: bfloat16 [3584, 4096], P(None, 'lat'), may hold values from -0.09375 to 0.09375
- enc_bias: float32 [4096], P('lat'), may hold values from -3 to 3
- dec_weight: bfloat16 [4096, 3584], P('lat'), may hold values from -0.375 to 0.375
- dec_bias: float32 [3584], replicated, may hold values from -3 to 3
Outputs:
- enc_grad: float32 [3584, 4096], P('rows', 'lat')
- dec_grad: float32 [4096, 3584], P('lat', 'rows')
- bias_grad: float32 [4096], P(('lat', 'rows'))
The draws below stay inside these ranges and needn't reach their ends.
Inputs may be any that keep to these rules, and one draw needn't show every extreme that they name: `block_ids`: each row names 2 different latent blocks. Among the 128 rows of one device (aligned blocks of 128 rows) no latent block is named by more than 12 rows, and on some device one block is named by exactly 12 rows.
All inputs are finite; a program needn't handle non-finite values.
Results may differ from the reference program's by a relative error of at most 0.0033.
Values may be sent and summed in bfloat16 or wider, within the bound.
No kernel may reach another device: no remote copies, remote signals or barrier semaphores. Data moves between devices by JAX's collectives and lax.ppermute only.
A program may use at most 64 MiB of HBM per device.

```python
import math
import jax
import jax.numpy as jnp
import numpy as np
from jax import lax

D = 3584
BLOCK = 128
K = 2
ROW_DEV = 128
NBLK = 32
LATENTS = 4096
CAP = 12
ROWS = 65536


def block_scale(stream_key, shape, split, least, largest):
    level = 1.0
    for dim, blocks in split:
        draws = jax.random.uniform(jax.random.fold_in(jax.random.fold_in(stream_key, 6), dim), (blocks,), jnp.float32, least / len(split), largest / len(split))
        level = level * jnp.repeat(jnp.exp(draws), shape[dim] // blocks).reshape((-1,) + (1,) * (len(shape) - 1 - dim))
    return level


def shared_out(own_key, own, number, rows, number_of, top, limit, lean):
    ranking = jax.random.permutation(own_key, number_of)
    packed, common = shares(number_of, rows * top, limit, lean, True), shares(number_of, rows * top, limit, lean, False)
    places = jnp.arange(number_of)

    def named(sizes, turn):
        used = int((sizes > 0).sum())
        fixed = max(1, used // 4)
        shifted = fixed + (places - fixed + turn * (used - fixed)) % max(1, number_of - fixed)
        return jnp.zeros((number_of,), jnp.int32).at[ranking[jnp.where(places < fixed, places, shifted)]].set(jnp.asarray(sizes, jnp.int32))

    sizes = jnp.where(number % 4 == 0, named(packed, number // 4), named(common, number - number // 4 - 1))
    mixed = jax.random.permutation(jax.random.fold_in(own, 3), number_of)
    giver, receiver = mixed[0:number_of // 2 * 2:2], mixed[1:number_of // 2 * 2:2]
    room = jnp.minimum(sizes[giver] - 1, limit - sizes[receiver]) // 2
    room = jnp.where((giver == ranking[0]) | (receiver == ranking[0]) | (sizes[receiver] == 0), 0, jnp.maximum(room, 0))
    shifted = jax.random.randint(jax.random.fold_in(own, 4), (number_of // 2,), 0, 1 << 20) % (room + 1)
    sizes = sizes.at[giver].add(-shifted).at[receiver].add(shifted)
    items = jnp.searchsorted(jnp.cumsum(sizes), jnp.arange(rows * top), side="right").astype(jnp.int32)
    grid = items.reshape(top, rows).T
    grid = grid[jax.random.permutation(jax.random.fold_in(own, 1), rows)]
    turn = jax.random.randint(jax.random.fold_in(own, 2), (rows, 1), 0, top)
    return jnp.take_along_axis(grid, (jnp.arange(top)[None, :] + turn) % top, axis=1)


def shares(amount, total, bound, lean, full):
    weights = [(1 << 20) // math.isqrt(rank ** lean) + 1 for rank in range(1, amount + 1)]
    largest = bound if full else min(bound, max(-(-total // amount), total * weights[0] // sum(weights)))
    least = 1 if total - largest >= amount - 1 else 0
    given, rest = [largest] + [least] * (amount - 1), total - largest - least * (amount - 1)
    while rest > 0:
        candidates = [i for i in range(1, amount) if given[i] < largest] or [i for i in range(1, amount) if given[i] < bound]
        mass, left = sum([weights[i] for i in candidates]), rest
        for i in candidates:
            more = min(bound - given[i], max(1, left * weights[i] // mass), rest)
            given[i] = given[i] + more
            rest = rest - more
    return np.array(given)


def bell_draw(rng, shape, deviation, reach, pieces=(), kind=jnp.bfloat16):
    array = jax.random.normal(rng, shape, jnp.float32) * deviation
    if len(pieces) > 0:
        array = block_scale(rng, shape, pieces, -0.22, 0.18) * array
    return jnp.clip(array, min=-reach, max=reach).astype(kind)


def setup_inputs(seed: int = 0) -> dict:
    arg_keys = jax.random.split(jax.random.key(seed), 7)
    activations = bell_draw(arg_keys[0], (ROWS, D), 1.0, 6.0, ((0, 512),))
    block_ids_keys = jax.random.split(jax.random.fold_in(arg_keys[1], 1), ROWS // ROW_DEV)
    block_ids_turns = jax.random.permutation(jax.random.fold_in(arg_keys[1], 3), ROWS // ROW_DEV)
    block_ids = jax.vmap(lambda own, number: shared_out(jax.random.fold_in(arg_keys[1], 2), own, number, ROW_DEV, NBLK, K, CAP, 2))(block_ids_keys, block_ids_turns).reshape((ROWS, K))
    enc_weight = bell_draw(arg_keys[2], (D, LATENTS), D ** -0.5, 0.09375, ((1, 32),))
    enc_bias = bell_draw(arg_keys[3], (LATENTS,), 0.5, 3.0, ((0, 32),), jnp.float32)
    dec_weight = bell_draw(arg_keys[4], (LATENTS, D), (BLOCK * K) ** -0.5, 0.375, ((0, 32),))
    dec_bias = bell_draw(arg_keys[5], (D,), 0.5, 3.0, (), jnp.float32)
    return dict(activations=activations, block_ids=block_ids, enc_weight=enc_weight, enc_bias=enc_bias, dec_weight=dec_weight, dec_bias=dec_bias)


def swish_grad(grad_in, pre_act):
    gate_sig = jax.nn.sigmoid(pre_act)
    return grad_in * gate_sig * (1.0 + pre_act * (1.0 - gate_sig))

def contract_first(left, right):
    return lax.dot_general(left.astype(jnp.float32), right.astype(jnp.float32), (((0,), (0,)), ((), ())))

def reference(activations, block_ids, enc_weight, enc_bias, dec_weight, dec_bias):
    most = ROWS // ROW_DEV * CAP
    padded = jnp.concatenate([activations, jnp.zeros((1, D), activations.dtype)], axis=0)

    def members(block_no):
        chosen = jnp.any(block_ids == block_no, axis=1)
        return jnp.nonzero(chosen, size=most, fill_value=ROWS)[0].astype(jnp.int32)

    def encode(block_no):
        picked_ids = members(block_no)
        picked = padded[picked_ids]
        first = block_no * BLOCK
        enc_cols = lax.dynamic_slice_in_dim(enc_weight, first, BLOCK, 1)
        bias_cols = lax.dynamic_slice_in_dim(enc_bias, first, BLOCK, 0)
        dec_rows = lax.dynamic_slice_in_dim(dec_weight, first, BLOCK, 0)
        pre_act = jnp.dot(picked, enc_cols, preferred_element_type=jnp.float32) + bias_cols
        latent_codes = (pre_act * jax.nn.sigmoid(pre_act)).astype(jnp.bfloat16)
        return (picked_ids, picked, pre_act, latent_codes, dec_rows)

    def add_block(rebuilt, block_no):
        picked_ids, picked, pre_act, latent_codes, dec_rows = encode(block_no)
        decoded = jnp.dot(latent_codes, dec_rows, preferred_element_type=jnp.float32).astype(jnp.bfloat16)
        return (rebuilt.at[picked_ids].add(decoded.astype(jnp.float32), mode='drop'), None)
    numbers = jnp.arange(NBLK, dtype=jnp.int32)
    initial = jnp.zeros((ROWS, D), jnp.float32) + dec_bias
    rebuilt = lax.scan(add_block, initial, numbers)[0]
    errors = ((rebuilt - activations.astype(jnp.float32)) / 64.0).astype(jnp.bfloat16)
    err_pad = jnp.concatenate([errors, jnp.zeros((1, D), errors.dtype)], axis=0)

    def block_grads(block_no):
        picked_ids, picked, pre_act, latent_codes, dec_rows = encode(block_no)
        picked_errs = err_pad[picked_ids]
        code_grad = lax.dot_general(picked_errs.astype(jnp.float32), dec_rows.astype(jnp.float32), (((1,), (1,)), ((), ())))
        grad_pre = swish_grad(code_grad, pre_act).astype(jnp.bfloat16)
        enc_part = contract_first(picked, grad_pre)
        dec_part = contract_first(latent_codes, picked_errs)
        bias_part = lax.optimization_barrier(jnp.sum(grad_pre.astype(jnp.float32), axis=0))
        return (enc_part, dec_part, bias_part)
    enc_all, dec_all, bias_all = lax.map(block_grads, numbers)
    enc_grad = jnp.transpose(enc_all, (1, 0, 2)).reshape(D, LATENTS)
    return (enc_grad, dec_all.reshape(LATENTS, D), bias_all.reshape(LATENTS))
```

```python
import functools

import jax
import jax.numpy as jnp
from jax import lax
from jax.experimental import pallas as pl
from jax.experimental.pallas import tpu as pltpu
from jax.sharding import PartitionSpec as P

CAP = 12
PAIR = 2 * CAP
BF = jnp.bfloat16
F32 = jnp.float32
VMEM = 56 * 1024 * 1024


def place_of(rows, first):
    row = lax.broadcasted_iota(jnp.int32, (rows, 1), 0) + first
    block = lax.shift_right_logical(row * 2731, 16)
    return block, row - block * PAIR


def left_rows(rows):
    _, place = place_of(rows, 0)
    return place < CAP


def dot(a, b):
    return lax.dot_general(a, b, (((1,), (0,)), ((), ())), preferred_element_type=F32)


def dot_t(a, b):
    return lax.dot_general(a, b, (((0,), (0,)), ((), ())), preferred_element_type=F32)


def dot_nt(a, b):
    return lax.dot_general(a, b, (((1,), (1,)), ((), ())), preferred_element_type=F32)


def split_halves(x, left):
    zero = jnp.zeros_like(x)
    return jnp.concatenate([jnp.where(left, x, zero), jnp.where(left, zero, x)], axis=1)


def join_halves(y, left):
    rows, n = y.shape[0], y.shape[1] // 2
    yl, yr = y[:, :n], y[:, n:]
    after = pltpu.roll(yr, rows - CAP, 0)
    before = pltpu.roll(yl, CAP, 0)
    return jnp.where(left, yl + after, yr + before)


def one_hot_slots(ids, blocks, first, rows):
    n = ids.shape[1]
    number = lax.broadcasted_iota(jnp.int32, (blocks, n), 0)
    member = (number == ids[0:1, :]) | (number == ids[1:2, :])
    earlier = (
        lax.broadcasted_iota(jnp.int32, (n, n), 0) < lax.broadcasted_iota(jnp.int32, (n, n), 1)
    )
    position = dot(member.astype(F32).astype(BF), earlier.astype(F32).astype(BF))
    code = jnp.where(member, position, 200.0).astype(BF)
    block, place = place_of(rows, first)
    left = place < CAP
    slot = (place - jnp.where(left, 0, CAP)).astype(F32)
    expand = lax.broadcasted_iota(jnp.int32, (rows, blocks), 1) == block
    spread = dot(expand.astype(F32).astype(BF), code)
    hit = (spread == slot).astype(F32)
    return split_halves(hit, left).astype(BF)


def pack_kernel(blocks, step, ids_ref, act_ref, out_ref, act2):
    rows = out_ref.shape[0]
    half = act_ref.shape[1] // 2
    n = act_ref.shape[0]

    @pl.when(pl.program_id(0) == 0)
    def _():
        act2[:n, :] = act_ref[:, :half]
        act2[n:, :] = act_ref[:, half:]

    sel = one_hot_slots(ids_ref[...], blocks, pl.program_id(0) * rows, rows)
    for c in range(0, half, step):
        out_ref[:, c : c + step] = dot(sel, act2[:, c : c + step]).astype(BF)


def pack(ids, act, blocks):
    n, width = act.shape
    half = width // 2
    total = blocks * PAIR
    rows = total // 4
    return pl.pallas_call(
        functools.partial(pack_kernel, blocks, 256),
        grid=(total // rows,),
        in_specs=[
            pl.BlockSpec(ids.shape, lambda i: (0, 0)),
            pl.BlockSpec(act.shape, lambda i: (0, 0)),
        ],
        out_specs=pl.BlockSpec((rows, half), lambda i: (i, 0)),
        out_shape=jax.ShapeDtypeStruct((total, half), BF),
        scratch_shapes=[pltpu.VMEM((2 * n, half), BF)],
        compiler_params=pltpu.CompilerParams(vmem_limit_bytes=VMEM),
        name="pack_rows",
    )(ids, act)


def code_kernel(step, x_ref, enc_ref, bias_ref, dec_ref, out_ref, pre_ref, enc2, dec2):
    rows, half = x_ref.shape
    n = enc_ref.shape[1]

    @pl.when(pl.program_id(0) == 0)
    def _():
        enc2[:, :n] = enc_ref[:half, :]
        enc2[:, n:] = enc_ref[half:, :]
        dec2[:n, :] = dec_ref[:, :half]
        dec2[n:, :] = dec_ref[:, half:]

    left = left_rows(rows)
    pre = join_halves(dot(x_ref[...], enc2[...]), left) + bias_ref[...]
    pre_ref[...] = pre
    codes = split_halves(pre * jax.nn.sigmoid(pre), left).astype(BF)
    for c in range(0, half, step):
        out_ref[:, c : c + step] = dot(codes, dec2[:, c : c + step]).astype(BF)


def encode_decode(x, enc, bias, dec):
    total, half = x.shape
    n = enc.shape[1]
    rows = total // 4
    return pl.pallas_call(
        functools.partial(code_kernel, 256),
        grid=(total // rows,),
        in_specs=[
            pl.BlockSpec((rows, half), lambda i: (i, 0)),
            pl.BlockSpec(enc.shape, lambda i: (0, 0)),
            pl.BlockSpec((1, n), lambda i: (0, 0)),
            pl.BlockSpec(dec.shape, lambda i: (0, 0)),
        ],
        out_specs=[
            pl.BlockSpec((rows, half), lambda i: (i, 0)),
            pl.BlockSpec((rows, n), lambda i: (i, 0)),
        ],
        out_shape=[
            jax.ShapeDtypeStruct((total, half), BF),
            jax.ShapeDtypeStruct((total, n), F32),
        ],
        scratch_shapes=[pltpu.VMEM((half, 2 * n), BF), pltpu.VMEM((2 * n, half), BF)],
        compiler_params=pltpu.CompilerParams(vmem_limit_bytes=VMEM),
        name="encode_decode",
    )(x, enc, bias, dec)


def error_kernel(blocks, ids_ref, parts_ref, al_ref, ar_ref, bl_ref, br_ref, out_ref, sel):
    total = parts_ref.shape[0]
    n = al_ref.shape[0]

    @pl.when(pl.program_id(0) == 0)
    def _():
        sel[...] = one_hot_slots(ids_ref[...], blocks, 0, total)

    sums = dot_t(sel[...], parts_ref[...])
    err_l = (sums[:n] + bl_ref[...] - al_ref[...].astype(F32)) * (1.0 / 64.0)
    err_r = (sums[n:] + br_ref[...] - ar_ref[...].astype(F32)) * (1.0 / 64.0)
    errors = jnp.concatenate([err_l.astype(BF), err_r.astype(BF)], axis=0)
    out_ref[...] = dot(sel[...], errors).astype(BF)


def error_rows(ids, parts, act, bias, blocks):
    total, half = parts.shape
    n = act.shape[0]
    step = 256
    steps = half // step
    return pl.pallas_call(
        functools.partial(error_kernel, blocks),
        grid=(steps,),
        in_specs=[
            pl.BlockSpec(ids.shape, lambda i: (0, 0)),
            pl.BlockSpec((total, step), lambda i: (0, i)),
            pl.BlockSpec((n, step), lambda i: (0, i)),
            pl.BlockSpec((n, step), lambda i: (0, i + steps)),
            pl.BlockSpec((1, step), lambda i: (0, i)),
            pl.BlockSpec((1, step), lambda i: (0, i + steps)),
        ],
        out_specs=pl.BlockSpec((total, step), lambda i: (0, i)),
        out_shape=jax.ShapeDtypeStruct((total, half), BF),
        scratch_shapes=[pltpu.VMEM((total, 2 * n), BF)],
        compiler_params=pltpu.CompilerParams(vmem_limit_bytes=VMEM),
        name="error_rows",
    )(ids, parts, act, act, bias, bias)


def hi_lo(x):
    hi = x.astype(BF).astype(F32)
    row = lax.broadcasted_iota(jnp.int32, (16, x.shape[1]), 0)
    return jnp.where(row == 0, hi, jnp.where(row == 1, x - hi, 0.0)).astype(BF)


def grad_kernel(x_ref, e_ref, pre_ref, dec_ref, out_ref, dec2):
    rows, half = x_ref.shape
    n = pre_ref.shape[1]
    groups, _, quarter = out_ref.shape
    dec2[:n, :] = dec_ref[:, :half]
    dec2[n:, :] = dec_ref[:, half:]
    left = left_rows(rows)
    pre = pre_ref[...]
    sig = jax.nn.sigmoid(pre)
    codes = split_halves(pre * sig, left).astype(BF)
    code_grad = join_halves(dot_nt(e_ref[...], dec2[...]), left)
    grad = (code_grad * sig * (1.0 + pre * (1.0 - sig))).astype(BF).astype(F32)
    grads = split_halves(grad, left)
    bias = jnp.sum(grads[:, :n], axis=0, keepdims=True)
    grads = grads.astype(BF)
    for g in range(0, groups // 2):
        cols = pl.ds(g * quarter, quarter)
        enc = dot_t(grads, x_ref[:, cols]).astype(BF)
        dec = dot_t(codes, e_ref[:, cols]).astype(BF)
        for s in range(2):
            out_ref[g + s * (groups // 2), :n, :] = enc[s * n : s * n + n]
            out_ref[g + s * (groups // 2), n : 2 * n, :] = dec[s * n : s * n + n]
    for g in range(groups):
        shifted = pltpu.roll(bias, (n - g * (n // groups)) % n, 1)
        out_ref[g, 2 * n :, :] = jnp.zeros((16, quarter), BF)
        out_ref[g, 2 * n :, :n] = hi_lo(shifted)


def gradients(x, err, pre, dec, groups):
    n, width = dec.shape
    return pl.pallas_call(
        grad_kernel,
        out_shape=jax.ShapeDtypeStruct((groups, 2 * n + 16, width // groups), BF),
        scratch_shapes=[pltpu.VMEM((2 * n, width // 2), BF)],
        compiler_params=pltpu.CompilerParams(vmem_limit_bytes=VMEM),
        name="gradients",
    )(x, err, pre, dec)


def first_sum_kernel(parts_ref, out_ref):
    groups, rows, quarter = parts_ref.shape
    n = (rows - 16) // 2
    chunks, out_rows, _ = out_ref.shape
    piece = out_rows - 16
    total = parts_ref[0, : 2 * n, :].astype(F32)
    bias = parts_ref[0, 2 * n :, :n].astype(F32)
    for g in range(1, groups):
        total = total + parts_ref[g, : 2 * n, :].astype(F32)
        bias = bias + parts_ref[g, 2 * n :, :n].astype(F32)
    turned = total.T.astype(BF)
    bias = jnp.sum(bias, axis=0, keepdims=True)
    for c in range(chunks):
        out_ref[c, :piece, :] = turned[c * piece : (c + 1) * piece]
        shifted = pltpu.roll(bias, (n - c * (n // 16)) % n, 1)
        out_ref[c, piece:, :n] = hi_lo(shifted)
        out_ref[c, piece:, n:] = jnp.zeros((16, n), BF)


def first_sum(parts, chunks):
    groups, rows, quarter = parts.shape
    return pl.pallas_call(
        first_sum_kernel,
        out_shape=jax.ShapeDtypeStruct((chunks, quarter // chunks + 16, rows - 16), BF),
        compiler_params=pltpu.CompilerParams(vmem_limit_bytes=VMEM),
        name="sum_over_y",
    )(parts)


def last_sum_kernel(parts_ref, enc_ref, dec_ref, bias_ref):
    groups, rows, cols = parts_ref.shape
    piece, n = rows - 16, cols // 2
    total = parts_ref[0].astype(F32)
    for g in range(1, groups):
        total = total + parts_ref[g].astype(F32)
    enc_ref[...] = total[:piece, :n]
    dec_ref[...] = total[:piece, n:]
    bias = jnp.sum(total[piece:, :n], axis=0, keepdims=True)
    bias_ref[...] = bias[:, : bias_ref.shape[1]]


def last_sum(parts, own):
    groups, rows, cols = parts.shape
    piece, n = rows - 16, cols // 2
    return pl.pallas_call(
        last_sum_kernel,
        out_shape=[
            jax.ShapeDtypeStruct((piece, n), F32),
            jax.ShapeDtypeStruct((piece, n), F32),
            jax.ShapeDtypeStruct((1, own), F32),
        ],
        compiler_params=pltpu.CompilerParams(vmem_limit_bytes=VMEM),
        name="sum_over_z",
    )(parts)


def exchange(x, blocks):
    shape = x.shape
    out = lax.all_to_all(
        x.reshape(blocks, shape[0] // blocks, shape[1]), "lat", split_axis=0, concat_axis=0, tiled=True
    )
    return out.reshape(shape)


def local(activations, block_ids, enc_weight, enc_bias, dec_weight, dec_bias):
    blocks = lax.axis_size("lat")
    parts_rows = lax.axis_size("rows")
    side = 4
    along_z = [[y * side + z for z in range(side)] for y in range(side)]
    along_y = [[y * side + z for y in range(side)] for z in range(side)]
    n = enc_weight.shape[1]
    ids = block_ids.T
    x = exchange(pack(ids, activations, blocks), blocks)
    decoded, pre = encode_decode(x, enc_weight, enc_bias[None, :], dec_weight)
    back = exchange(decoded, blocks)
    err = exchange(error_rows(ids, back, activations, dec_bias[None, :], blocks), blocks)
    terms = gradients(x, err, pre, dec_weight, side)
    terms = lax.all_to_all(
        terms, "rows", split_axis=0, concat_axis=0, axis_index_groups=along_y, tiled=True
    )
    terms = first_sum(terms, side)
    terms = lax.all_to_all(
        terms, "rows", split_axis=0, concat_axis=0, axis_index_groups=along_z, tiled=True
    )
    enc_grad, dec_turned, bias_grad = last_sum(terms, n // parts_rows)
    return enc_grad, dec_turned.T, bias_grad.reshape(-1)


def solution(mesh):
    in_specs = (
        P(("rows", "lat"), None),
        P(("rows", "lat"), None),
        P(None, "lat"),
        P("lat"),
        P("lat", None),
        P(),
    )
    out_specs = (P("rows", "lat"), P("lat", "rows"), P(("lat", "rows")))
    return jax.shard_map(local, mesh=mesh, in_specs=in_specs, out_specs=out_specs, check_vma=False)
```

```python
import functools

import jax
import jax.numpy as jnp
from jax import lax
from jax.experimental import pallas as pl
from jax.experimental.pallas import tpu as pltpu
from jax.sharding import PartitionSpec as P

CAP = 12
PAIR = 2 * CAP
BF = jnp.bfloat16
F32 = jnp.float32
VMEM = 56 * 1024 * 1024
SIDE = 4


def place_of(rows, first):
    row = lax.broadcasted_iota(jnp.int32, (rows, 1), 0) + first
    block = lax.shift_right_logical(row * 2731, 16)
    return block, row - block * PAIR


def left_rows(rows):
    _, place = place_of(rows, 0)
    return place < CAP


def dot(a, b):
    return lax.dot_general(a, b, (((1,), (0,)), ((), ())), preferred_element_type=F32)


def dot_t(a, b):
    return lax.dot_general(a, b, (((0,), (0,)), ((), ())), preferred_element_type=F32)


def dot_nt(a, b):
    return lax.dot_general(a, b, (((1,), (1,)), ((), ())), preferred_element_type=F32)


def split_halves(x, left):
    zero = jnp.zeros_like(x)
    return jnp.concatenate([jnp.where(left, x, zero), jnp.where(left, zero, x)], axis=1)


def join_halves(y, left):
    rows, n = y.shape[0], y.shape[1] // 2
    yl, yr = y[:, :n], y[:, n:]
    after = pltpu.roll(yr, rows - CAP, 0)
    before = pltpu.roll(yl, CAP, 0)
    return jnp.where(left, yl + after, yr + before)


def one_hot_slots(ids, blocks, first, rows):
    n = ids.shape[1]
    number = lax.broadcasted_iota(jnp.int32, (blocks, n), 0)
    member = (number == ids[0:1, :]) | (number == ids[1:2, :])
    earlier = (
        lax.broadcasted_iota(jnp.int32, (n, n), 0) < lax.broadcasted_iota(jnp.int32, (n, n), 1)
    )
    position = dot(member.astype(F32).astype(BF), earlier.astype(F32).astype(BF))
    code = jnp.where(member, position, 200.0).astype(BF)
    block, place = place_of(rows, first)
    left = place < CAP
    slot = (place - jnp.where(left, 0, CAP)).astype(F32)
    expand = lax.broadcasted_iota(jnp.int32, (rows, blocks), 1) == block
    spread = dot(expand.astype(F32).astype(BF), code)
    hit = (spread == slot).astype(F32)
    return split_halves(hit, left).astype(BF)


def pack_kernel(blocks, step, ids_ref, act_ref, out_ref, act2):
    rows = out_ref.shape[0]
    half = act_ref.shape[1] // 2
    n = act_ref.shape[0]

    @pl.when(pl.program_id(0) == 0)
    def _():
        act2[:n, :] = act_ref[:, :half]
        act2[n:, :] = act_ref[:, half:]

    sel = one_hot_slots(ids_ref[...], blocks, pl.program_id(0) * rows, rows)
    for c in range(0, half, step):
        out_ref[:, c : c + step] = dot(sel, act2[:, c : c + step]).astype(BF)


def pack(ids, act, blocks):
    n, width = act.shape
    half = width // 2
    total = blocks * PAIR
    rows = total // 4
    return pl.pallas_call(
        functools.partial(pack_kernel, blocks, 256),
        grid=(total // rows,),
        in_specs=[
            pl.BlockSpec(ids.shape, lambda i: (0, 0)),
            pl.BlockSpec(act.shape, lambda i: (0, 0)),
        ],
        out_specs=pl.BlockSpec((rows, half), lambda i: (i, 0)),
        out_shape=jax.ShapeDtypeStruct((total, half), BF),
        scratch_shapes=[pltpu.VMEM((2 * n, half), BF)],
        compiler_params=pltpu.CompilerParams(vmem_limit_bytes=VMEM),
        name="pack_rows",
    )(ids, act)


def code_kernel(step, x_ref, enc_ref, bias_ref, dec_ref, out_ref, pre_ref, enc2, dec2):
    rows, half = x_ref.shape
    n = enc_ref.shape[1]

    @pl.when(pl.program_id(0) == 0)
    def _():
        enc2[:, :n] = enc_ref[:half, :]
        enc2[:, n:] = enc_ref[half:, :]
        dec2[:n, :] = dec_ref[:, :half]
        dec2[n:, :] = dec_ref[:, half:]

    left = left_rows(rows)
    pre = join_halves(dot(x_ref[...], enc2[...]), left) + bias_ref[...]
    pre_ref[...] = pre
    codes = split_halves(pre * jax.nn.sigmoid(pre), left).astype(BF)
    for c in range(0, half, step):
        out_ref[:, c : c + step] = dot(codes, dec2[:, c : c + step]).astype(BF)


def encode_decode(x, enc, bias, dec):
    total, half = x.shape
    n = enc.shape[1]
    rows = total // 4
    return pl.pallas_call(
        functools.partial(code_kernel, 256),
        grid=(total // rows,),
        in_specs=[
            pl.BlockSpec((rows, half), lambda i: (i, 0)),
            pl.BlockSpec(enc.shape, lambda i: (0, 0)),
            pl.BlockSpec((1, n), lambda i: (0, 0)),
            pl.BlockSpec(dec.shape, lambda i: (0, 0)),
        ],
        out_specs=[
            pl.BlockSpec((rows, half), lambda i: (i, 0)),
            pl.BlockSpec((rows, n), lambda i: (i, 0)),
        ],
        out_shape=[
            jax.ShapeDtypeStruct((total, half), BF),
            jax.ShapeDtypeStruct((total, n), F32),
        ],
        scratch_shapes=[pltpu.VMEM((half, 2 * n), BF), pltpu.VMEM((2 * n, half), BF)],
        compiler_params=pltpu.CompilerParams(vmem_limit_bytes=VMEM),
        name="encode_decode",
    )(x, enc, bias, dec)


def error_kernel(blocks, ids_ref, parts_ref, al_ref, ar_ref, bl_ref, br_ref, out_ref, sel):
    total = parts_ref.shape[0]
    n = al_ref.shape[0]

    @pl.when(pl.program_id(0) == 0)
    def _():
        sel[...] = one_hot_slots(ids_ref[...], blocks, 0, total)

    sums = dot_t(sel[...], parts_ref[...])
    err_l = (sums[:n] + bl_ref[...] - al_ref[...].astype(F32)) * (1.0 / 64.0)
    err_r = (sums[n:] + br_ref[...] - ar_ref[...].astype(F32)) * (1.0 / 64.0)
    errors = jnp.concatenate([err_l.astype(BF), err_r.astype(BF)], axis=0)
    out_ref[...] = dot(sel[...], errors).astype(BF)


def error_rows(ids, parts, act, bias, blocks):
    total, half = parts.shape
    n = act.shape[0]
    step = 256
    steps = half // step
    return pl.pallas_call(
        functools.partial(error_kernel, blocks),
        grid=(steps,),
        in_specs=[
            pl.BlockSpec(ids.shape, lambda i: (0, 0)),
            pl.BlockSpec((total, step), lambda i: (0, i)),
            pl.BlockSpec((n, step), lambda i: (0, i)),
            pl.BlockSpec((n, step), lambda i: (0, i + steps)),
            pl.BlockSpec((1, step), lambda i: (0, i)),
            pl.BlockSpec((1, step), lambda i: (0, i + steps)),
        ],
        out_specs=pl.BlockSpec((total, step), lambda i: (0, i)),
        out_shape=jax.ShapeDtypeStruct((total, half), BF),
        scratch_shapes=[pltpu.VMEM((total, 2 * n), BF)],
        compiler_params=pltpu.CompilerParams(vmem_limit_bytes=VMEM),
        name="error_rows",
    )(ids, parts, act, act, bias, bias)


def hi_lo(x):
    hi = x.astype(BF).astype(F32)
    row = lax.broadcasted_iota(jnp.int32, (16, x.shape[1]), 0)
    return jnp.where(row == 0, hi, jnp.where(row == 1, x - hi, 0.0)).astype(BF)


def grad_kernel(x_ref, e_ref, pre_ref, dec_ref, *refs):
    outs, (dec2, pieces, sems) = refs[:-3], refs[-3:]
    rows, half = x_ref.shape
    n = pre_ref.shape[1]
    groups, _, quarter = pieces.shape
    me = lax.axis_index("rows") // SIDE
    dec2[:n, :] = dec_ref[:, :half]
    dec2[n:, :] = dec_ref[:, half:]
    left = left_rows(rows)
    pre = pre_ref[...]
    sig = jax.nn.sigmoid(pre)
    codes = split_halves(pre * sig, left).astype(BF)
    code_grad = join_halves(dot_nt(e_ref[...], dec2[...]), left)
    grad = (code_grad * sig * (1.0 + pre * (1.0 - sig))).astype(BF).astype(F32)
    grads = split_halves(grad, left)
    bias = jnp.sum(grads[:, :n], axis=0, keepdims=True)
    grads = grads.astype(BF)
    for g in range(0, groups // 2):
        cols = pl.ds(g * quarter, quarter)
        enc = dot_t(grads, x_ref[:, cols]).astype(BF)
        dec = dot_t(codes, e_ref[:, cols]).astype(BF)
        for s in range(2):
            pieces[g + s * (groups // 2), :n, :] = enc[s * n : s * n + n]
            pieces[g + s * (groups // 2), n : 2 * n, :] = dec[s * n : s * n + n]
    for g in range(groups):
        shifted = pltpu.roll(bias, (n - g * (n // groups)) % n, 1)
        pieces[g, 2 * n :, :] = jnp.zeros((16, quarter), BF)
        pieces[g, 2 * n :, :n] = hi_lo(shifted)
    hand_out(pieces, outs, me, sems)


def hand_out(pieces, outs, me, sems):
    copies = [
        pltpu.make_async_copy(pieces.at[lax.rem(me + k, SIDE)], out, sems.at[k])
        for k, out in enumerate(outs)
    ]
    for copy in copies:
        copy.start()
    for copy in copies:
        copy.wait()


def gradients(x, err, pre, dec):
    n, width = dec.shape
    piece = (2 * n + 16, width // SIDE)
    return pl.pallas_call(
        grad_kernel,
        out_shape=[jax.ShapeDtypeStruct(piece, BF)] * SIDE,
        out_specs=[pl.BlockSpec(memory_space=pl.ANY)] * SIDE,
        scratch_shapes=[
            pltpu.VMEM((2 * n, width // 2), BF),
            pltpu.VMEM((SIDE,) + piece, BF),
            pltpu.SemaphoreType.DMA((SIDE,)),
        ],
        compiler_params=pltpu.CompilerParams(vmem_limit_bytes=VMEM),
        name="gradients",
    )(x, err, pre, dec)


def first_sum_kernel(*refs):
    ins, outs, (pieces, sems) = refs[:SIDE], refs[SIDE : 2 * SIDE], refs[2 * SIDE :]
    rows, quarter = ins[0].shape
    n = (rows - 16) // 2
    piece = pieces.shape[1] - 16
    total = ins[0][: 2 * n, :].astype(F32)
    bias = ins[0][2 * n :, :n].astype(F32)
    for part in ins[1:]:
        total = total + part[: 2 * n, :].astype(F32)
        bias = bias + part[2 * n :, :n].astype(F32)
    turned = total.T.astype(BF)
    bias = jnp.sum(bias, axis=0, keepdims=True)
    for c in range(SIDE):
        pieces[c, :piece, :] = turned[c * piece : (c + 1) * piece]
        shifted = pltpu.roll(bias, (n - c * (n // (SIDE * SIDE))) % n, 1)
        pieces[c, piece:, :n] = hi_lo(shifted)
        pieces[c, piece:, n:] = jnp.zeros((16, n), BF)
    hand_out(pieces, outs, lax.rem(lax.axis_index("rows"), SIDE), sems)


def first_sum(parts):
    rows, quarter = parts[0].shape
    piece = (quarter // SIDE + 16, rows - 16)
    return pl.pallas_call(
        first_sum_kernel,
        out_shape=[jax.ShapeDtypeStruct(piece, BF)] * SIDE,
        out_specs=[pl.BlockSpec(memory_space=pl.ANY)] * SIDE,
        scratch_shapes=[pltpu.VMEM((SIDE,) + piece, BF), pltpu.SemaphoreType.DMA((SIDE,))],
        compiler_params=pltpu.CompilerParams(vmem_limit_bytes=VMEM),
        name="sum_over_y",
    )(*parts)


def last_sum_kernel(*refs):
    ins, (enc_ref, dec_ref, bias_ref) = refs[:SIDE], refs[SIDE:]
    rows, cols = ins[0].shape
    piece, n = rows - 16, cols // 2
    total = ins[0][...].astype(F32)
    for part in ins[1:]:
        total = total + part[...].astype(F32)
    enc_ref[...] = total[:piece, :n]
    dec_ref[...] = total[:piece, n:]
    bias = jnp.sum(total[piece:, :n], axis=0, keepdims=True)
    bias_ref[...] = bias[:, : bias_ref.shape[1]]


def last_sum(parts, own):
    rows, cols = parts[0].shape
    piece, n = rows - 16, cols // 2
    return pl.pallas_call(
        last_sum_kernel,
        out_shape=[
            jax.ShapeDtypeStruct((piece, n), F32),
            jax.ShapeDtypeStruct((piece, n), F32),
            jax.ShapeDtypeStruct((1, own), F32),
        ],
        compiler_params=pltpu.CompilerParams(vmem_limit_bytes=VMEM),
        name="sum_over_z",
    )(*parts)


def swap_pieces(pieces, along_y):
    got = [pieces[0]]
    for k in (1, 3, 2):
        pairs = []
        for i in range(SIDE * SIDE):
            y, z = divmod(i, SIDE)
            to = ((y + k) % SIDE, z) if along_y else (y, (z + k) % SIDE)
            pairs.append((i, to[0] * SIDE + to[1]))
        got.append(lax.ppermute(pieces[k], "rows", pairs))
    return got


def exchange(x, blocks):
    shape = x.shape
    out = lax.all_to_all(
        x.reshape(blocks, shape[0] // blocks, shape[1]), "lat", split_axis=0, concat_axis=0, tiled=True
    )
    return out.reshape(shape)


def local(activations, block_ids, enc_weight, enc_bias, dec_weight, dec_bias):
    blocks = lax.axis_size("lat")
    parts_rows = lax.axis_size("rows")
    n = enc_weight.shape[1]
    ids = block_ids.T
    x = exchange(pack(ids, activations, blocks), blocks)
    decoded, pre = encode_decode(x, enc_weight, enc_bias[None, :], dec_weight)
    back = exchange(decoded, blocks)
    err = exchange(error_rows(ids, back, activations, dec_bias[None, :], blocks), blocks)
    terms = swap_pieces(gradients(x, err, pre, dec_weight), True)
    terms = swap_pieces(first_sum(terms), False)
    enc_grad, dec_turned, bias_grad = last_sum(terms, n // parts_rows)
    return enc_grad, dec_turned.T, bias_grad.reshape(-1)


def solution(mesh):
    in_specs = (
        P(("rows", "lat"), None),
        P(("rows", "lat"), None),
        P(None, "lat"),
        P("lat"),
        P("lat", None),
        P(),
    )
    out_specs = (P("rows", "lat"), P("lat", "rows"), P(("lat", "rows")))
    return jax.shard_map(local, mesh=mesh, in_specs=in_specs, out_specs=out_specs, check_vma=False)
```

```python
import functools

import jax
import jax.numpy as jnp
from jax import lax
from jax.experimental import pallas as pl
from jax.experimental.pallas import tpu as pltpu
from jax.sharding import PartitionSpec as P

SLOTS = 6
PAIR = 2 * SLOTS
SIDE = 4
STEPS = (0, 1, 2, -2, -1)
BF = jnp.bfloat16
F32 = jnp.float32
VMEM = 56 * 1024 * 1024
PARAMS = pltpu.CompilerParams(vmem_limit_bytes=VMEM)
ANY = pl.BlockSpec(memory_space=pl.ANY)


def by_twelve(row):
    return lax.shift_right_logical(row * 5462, 16)


def dot(a, b):
    return lax.dot_general(a, b, (((1,), (0,)), ((), ())), preferred_element_type=F32)


def dot_t(a, b):
    return lax.dot_general(a, b, (((0,), (0,)), ((), ())), preferred_element_type=F32)


def dot_nt(a, b):
    return lax.dot_general(a, b, (((1,), (1,)), ((), ())), preferred_element_type=F32)


def left_rows(rows):
    row = lax.broadcasted_iota(jnp.int32, (rows, 1), 0)
    return row - by_twelve(row) * PAIR < SLOTS


def split_halves(x, left):
    zero = jnp.zeros_like(x)
    return jnp.concatenate([jnp.where(left, x, zero), jnp.where(left, zero, x)], axis=1)


def join_halves(y, left):
    rows, n = y.shape[0], y.shape[1] // 2
    yl, yr = y[:, :n], y[:, n:]
    after = pltpu.roll(yr, rows - SLOTS, 0)
    before = pltpu.roll(yl, SLOTS, 0)
    return jnp.where(left, yl + after, yr + before)


def one_hot_slots(ids, blocks):
    n = ids.shape[1]
    rows = 2 * blocks * PAIR
    number = lax.broadcasted_iota(jnp.int32, (blocks, n), 0)
    member = (number == ids[0:1, :]) | (number == ids[1:2, :])
    earlier = (
        lax.broadcasted_iota(jnp.int32, (n, n), 0) < lax.broadcasted_iota(jnp.int32, (n, n), 1)
    )
    position = dot(member.astype(F32).astype(BF), earlier.astype(F32).astype(BF))
    code = jnp.where(member, position, 200.0).astype(BF)
    zl = lax.rem(lax.axis_index("lat") // 2, SIDE)
    row = lax.broadcasted_iota(jnp.int32, (rows, 1), 0)
    piece = by_twelve(row)
    place = row - piece * PAIR
    first = piece < blocks
    in_a, in_b = piece, piece - blocks
    xc = jnp.where(first, in_a & 7, lax.shift_right_logical(in_b, 2))
    k = jnp.where(first, lax.shift_right_logical(in_a, 3), in_b & 3)
    block = lax.shift_right_logical(xc, 1) * (2 * SIDE) + ((zl + k) & 3) * 2 + (xc & 1)
    left = place < SLOTS
    slot = place - jnp.where(left, 0, SLOTS) + jnp.where(first, 0, SLOTS)
    expand = lax.broadcasted_iota(jnp.int32, (rows, blocks), 1) == block
    spread = dot(expand.astype(F32).astype(BF), code)
    hit = (spread == slot.astype(F32)).astype(F32)
    return split_halves(hit, left).astype(BF)


def start(pairs, sems, first=0):
    copies = [pltpu.make_async_copy(a, b, sems.at[first + i]) for i, (a, b) in enumerate(pairs)]
    for copy in copies:
        copy.start()
    return copies


def wait(copies):
    for copy in copies:
        copy.wait()


def five_moves(refs, k, first, rows, other):
    if k != 2:
        return [(refs[k if k < 2 else 4].at[first : first + rows], other)]
    part = refs[2].shape[0]
    return [
        (refs[2 + h], other.at[h * part - first : (h + 1) * part - first])
        for h in range(2)
        if first <= h * part < first + rows
    ]


def flip(pairs):
    return [(b, a) for a, b in pairs]


def send_slots(sel, rows2, pieces, outs, sems):
    part = pieces.shape[1]
    copies = []
    for i in range(2 * SIDE):
        pieces[i] = dot(sel[i * part : (i + 1) * part, :], rows2[...]).astype(BF)
        if i < SIDE:
            pairs = flip(five_moves(outs, i, 0, part, pieces.at[i]))
        else:
            pairs = [(pieces.at[i], outs[5].at[(i - SIDE) * part : (i - SIDE + 1) * part])]
        copies += start(pairs, sems, 2 * i)
    wait(copies)


def five_shapes(total, half):
    part = total // SIDE
    rows = [part, part, part // 2, part // 2, part]
    return [jax.ShapeDtypeStruct((r, half), BF) for r in rows]


def slot_shapes(blocks, half):
    total = blocks * PAIR
    return five_shapes(total, half) + [jax.ShapeDtypeStruct((total, half), BF)]


def pack_kernel(blocks, ids_ref, act_ref, *refs):
    outs, (act2, sel, pieces, in_sems, sems) = refs[:6], refs[6:]
    n, width = act_ref.shape
    half = width // 2
    copies = start(
        [(act_ref.at[:, s * half : (s + 1) * half], act2.at[s * n : (s + 1) * n]) for s in range(2)],
        in_sems,
    )
    sel[...] = one_hot_slots(ids_ref[...], blocks)
    wait(copies)
    send_slots(sel, act2, pieces, outs, sems)


def pack(ids, act, blocks):
    n, width = act.shape
    half = width // 2
    part = blocks * PAIR // SIDE
    return pl.pallas_call(
        functools.partial(pack_kernel, blocks),
        in_specs=[pl.BlockSpec(memory_space=pltpu.VMEM), ANY],
        out_specs=[ANY] * 6,
        out_shape=slot_shapes(blocks, half),
        scratch_shapes=[
            pltpu.VMEM((2 * n, half), BF),
            pltpu.VMEM((2 * SIDE * part, 2 * n), BF),
            pltpu.VMEM((2 * SIDE, part, half), BF),
            pltpu.SemaphoreType.DMA((2,)),
            pltpu.SemaphoreType.DMA((4 * SIDE,)),
        ],
        compiler_params=PARAMS,
        name="pack_rows",
    )(ids, act)


def swap_kernel(merge, *refs):
    if merge:
        ins, out_ref, (pieces, done, in_sems, sems) = refs[:5], refs[5], refs[6:]
    else:
        in_ref, outs, (pieces, done, in_sems, sems) = refs[0], refs[1:6], refs[6:]
    rows = pieces.shape[1]
    part = rows // SIDE
    halves = range(2)

    def by_step(arrays, buffer, h):
        pairs = []
        for k in range(SIDE):
            pairs += five_moves(arrays, k, h * part, part, buffer.at[h, k * part : (k + 1) * part])
        return pairs

    if merge:
        moves = [by_step(ins, pieces, h) for h in halves]
    else:
        moves = [[(in_ref.at[h * rows : (h + 1) * rows], pieces.at[h])] for h in halves]
    copies = [start(moves[h], in_sems, h * SIDE) for h in halves]
    row = lax.broadcasted_iota(jnp.int32, (rows, 1), 0)
    piece = by_twelve(row)
    source = (piece & 3) * part + lax.shift_right_logical(piece, 2) * PAIR + row - piece * PAIR
    turn = (lax.broadcasted_iota(jnp.int32, (rows, rows), 1) == source).astype(F32).astype(BF)
    sent = []
    for h in halves:
        wait(copies[h])
        done[h] = dot(turn, pieces[h]).astype(BF)
        if merge:
            sent += start([(done.at[h], out_ref.at[h * rows : (h + 1) * rows])], sems, h * SIDE)
        else:
            sent += start(flip(by_step(outs, done, h)), sems, h * SIDE)
    wait(sent)


def swap_pieces(arrays, merge):
    total = sum(a.shape[0] for a in arrays)
    half = arrays[0].shape[1]
    return pl.pallas_call(
        functools.partial(swap_kernel, merge),
        in_specs=[ANY] * len(arrays),
        out_specs=ANY if merge else [ANY] * 5,
        out_shape=jax.ShapeDtypeStruct((total, half), BF) if merge else five_shapes(total, half),
        scratch_shapes=[
            pltpu.VMEM((2, total // 2, half), BF),
            pltpu.VMEM((2, total // 2, half), BF),
            pltpu.SemaphoreType.DMA((4 * SIDE,)),
            pltpu.SemaphoreType.DMA((4 * SIDE,)),
        ],
        compiler_params=PARAMS,
        name="merge_pieces" if merge else "split_pieces",
    )(*arrays)


def code_kernel(parts, *refs):
    ins, (enc_ref, bias_ref, dec_ref) = refs[:parts], refs[parts : parts + 3]
    outs, pre_ref = refs[parts + 3 : 2 * parts + 3], refs[2 * parts + 3]
    enc2, dec2, x, done, w_sems, in_sems, sems = refs[2 * parts + 4 :]
    half, n = enc2.shape[0], enc2.shape[1] // 2
    rows = x.shape[1]

    def piece(refs, i, buffer):
        if parts == 1:
            return [(refs[0].at[i * rows : (i + 1) * rows], buffer.at[i])]
        return five_moves(refs, i, 0, rows, buffer.at[i])

    enc_copies = start(
        [(enc_ref.at[s * half : (s + 1) * half], enc2.at[:, s * n : (s + 1) * n]) for s in range(2)],
        w_sems,
    )
    in_copies = [start(piece(ins, i, x), in_sems, 2 * i) for i in range(SIDE)]
    dec_copies = start(
        [(dec_ref.at[:, s * half : (s + 1) * half], dec2.at[s * n : (s + 1) * n]) for s in range(2)],
        w_sems,
        2,
    )
    left = left_rows(rows)
    wait(enc_copies)
    sent = []
    for i in range(SIDE):
        wait(in_copies[i])
        pre = join_halves(dot(x[i], enc2[...]), left) + bias_ref[...]
        pre_ref[i * rows : (i + 1) * rows, :] = pre
        codes = split_halves(pre * jax.nn.sigmoid(pre), left).astype(BF)
        if i == 0:
            wait(dec_copies)
        done[i] = dot(codes, dec2[...]).astype(BF)
        sent += start(flip(piece(outs, i, done)), sems, 2 * i)
    wait(sent)


def encode_decode(x, enc, bias, dec):
    width, n = enc.shape
    half = width // 2
    parts = len(x)
    total = sum(a.shape[0] for a in x)
    rows = total // SIDE
    return pl.pallas_call(
        functools.partial(code_kernel, parts),
        in_specs=[ANY] * (parts + 1) + [pl.BlockSpec(memory_space=pltpu.VMEM), ANY],
        out_specs=[ANY] * parts + [pl.BlockSpec(memory_space=pltpu.VMEM)],
        out_shape=[jax.ShapeDtypeStruct(a.shape, BF) for a in x]
        + [jax.ShapeDtypeStruct((total, n), F32)],
        scratch_shapes=[
            pltpu.VMEM((half, 2 * n), BF),
            pltpu.VMEM((2 * n, half), BF),
            pltpu.VMEM((SIDE, rows, half), BF),
            pltpu.VMEM((SIDE, rows, half), BF),
            pltpu.SemaphoreType.DMA((4,)),
            pltpu.SemaphoreType.DMA((2 * SIDE,)),
            pltpu.SemaphoreType.DMA((2 * SIDE,)),
        ],
        compiler_params=PARAMS,
        name="encode_decode",
    )(*x, enc, bias, dec)


def slot_moves(refs, buffer):
    part = refs[0].shape[0]
    pairs = []
    for k in range(SIDE):
        pairs += five_moves(refs, k, 0, part, buffer.at[k * part : (k + 1) * part])
    return pairs + [(refs[5], buffer.at[SIDE * part :])]


def error_kernel(blocks, ids_ref, bias_ref, act_ref, *refs):
    ins, outs = refs[:6], refs[6:12]
    act2, back, sel, err2, pieces, act_sems, in_sems, sems = refs[12:]
    n, width = act_ref.shape
    half = width // 2
    copies = start(slot_moves(ins, back), in_sems)
    copies += start(
        [(act_ref.at[:, s * half : (s + 1) * half], act2.at[s * n : (s + 1) * n]) for s in range(2)],
        act_sems,
    )
    sel[...] = one_hot_slots(ids_ref[...], blocks)
    wait(copies)
    step = 256
    for c in range(0, half, step):
        sums = dot_t(sel[...], back[:, c : c + step])
        for s in range(2):
            rows = slice(s * n, (s + 1) * n)
            bias = bias_ref[:, s * half + c : s * half + c + step]
            wanted = act2[rows, c : c + step].astype(F32)
            err2[rows, c : c + step] = ((sums[rows] + bias - wanted) * (1.0 / 64.0)).astype(BF)
    send_slots(sel, err2, pieces, outs, sems)


def error_rows(ids, back, act, bias, blocks):
    n, width = act.shape
    half = width // 2
    total = 2 * blocks * PAIR
    part = total // (2 * SIDE)
    in_vmem = pl.BlockSpec(memory_space=pltpu.VMEM)
    return pl.pallas_call(
        functools.partial(error_kernel, blocks),
        in_specs=[in_vmem, in_vmem] + [ANY] * 7,
        out_specs=[ANY] * 6,
        out_shape=slot_shapes(blocks, half),
        scratch_shapes=[
            pltpu.VMEM((2 * n, half), BF),
            pltpu.VMEM((total, half), BF),
            pltpu.VMEM((total, 2 * n), BF),
            pltpu.VMEM((2 * n, half), BF),
            pltpu.VMEM((2 * SIDE, part, half), BF),
            pltpu.SemaphoreType.DMA((2,)),
            pltpu.SemaphoreType.DMA((6,)),
            pltpu.SemaphoreType.DMA((4 * SIDE,)),
        ],
        compiler_params=PARAMS,
        name="error_rows",
    )(ids, bias, act, *back)


def hi_lo(x):
    hi = x.astype(BF).astype(F32)
    row = lax.broadcasted_iota(jnp.int32, (16, x.shape[1]), 0)
    return jnp.where(row == 0, hi, jnp.where(row == 1, x - hi, 0.0)).astype(BF)


def grad_kernel(pre_a, pre_b, dec_ref, *refs):
    x_refs, e_refs, outs = refs[:6], refs[6:12], refs[12:16]
    dec2, x, e, pieces, w_sems, x_sems, e_sems, sems = refs[16:]
    rows, half = x.shape
    n = pre_a.shape[1]
    groups, _, quarter = pieces.shape
    dec_copies = start(
        [(dec_ref.at[:, s * half : (s + 1) * half], dec2.at[s * n : (s + 1) * n]) for s in range(2)],
        w_sems,
    )
    e_copies = start(slot_moves(e_refs, e), e_sems)
    x_copies = start(slot_moves(x_refs, x), x_sems)
    me = lax.axis_index("rows") // SIDE
    left = left_rows(rows)
    pre = jnp.concatenate([pre_b[...], pre_a[...]], axis=0)
    sig = jax.nn.sigmoid(pre)
    codes = split_halves(pre * sig, left).astype(BF)
    wait(dec_copies)
    wait(e_copies)
    code_grad = join_halves(dot_nt(e[...], dec2[...]), left)
    grad = (code_grad * sig * (1.0 + pre * (1.0 - sig))).astype(BF).astype(F32)
    grads = split_halves(grad, left)
    bias = jnp.sum(grads[:, :n], axis=0, keepdims=True)
    grads = grads.astype(BF)
    wait(x_copies)
    for g in range(0, groups // 2):
        cols = pl.ds(g * quarter, quarter)
        enc = dot_t(grads, x[:, cols]).astype(BF)
        dec = dot_t(codes, e[:, cols]).astype(BF)
        for s in range(2):
            pieces[g + s * (groups // 2), :n, :] = enc[s * n : s * n + n]
            pieces[g + s * (groups // 2), n : 2 * n, :] = dec[s * n : s * n + n]
    for g in range(groups):
        shifted = pltpu.roll(bias, (n - g * (n // groups)) % n, 1)
        pieces[g, 2 * n :, :] = jnp.zeros((16, quarter), BF)
        pieces[g, 2 * n :, :n] = hi_lo(shifted)
    hand_out(pieces, outs, me, sems)


def hand_out(pieces, outs, me, sems):
    wait(start([(pieces.at[lax.rem(me + k, SIDE)], out) for k, out in enumerate(outs)], sems))


def gradients(x, err, pre_a, pre_b, dec):
    n, width = dec.shape
    piece = (2 * n + 16, width // SIDE)
    rows = 2 * pre_a.shape[0]
    in_vmem = pl.BlockSpec(memory_space=pltpu.VMEM)
    return pl.pallas_call(
        grad_kernel,
        in_specs=[in_vmem, in_vmem] + [ANY] * 13,
        out_shape=[jax.ShapeDtypeStruct(piece, BF)] * SIDE,
        out_specs=[ANY] * SIDE,
        scratch_shapes=[
            pltpu.VMEM((2 * n, width // 2), BF),
            pltpu.VMEM((rows, width // 2), BF),
            pltpu.VMEM((rows, width // 2), BF),
            pltpu.VMEM((SIDE,) + piece, BF),
            pltpu.SemaphoreType.DMA((2,)),
            pltpu.SemaphoreType.DMA((6,)),
            pltpu.SemaphoreType.DMA((6,)),
            pltpu.SemaphoreType.DMA((SIDE,)),
        ],
        compiler_params=PARAMS,
        name="gradients",
    )(pre_a, pre_b, dec, *x, *err)


def first_sum_kernel(*refs):
    ins, outs, (pieces, sems) = refs[:SIDE], refs[SIDE : 2 * SIDE], refs[2 * SIDE :]
    rows, quarter = ins[0].shape
    n = (rows - 16) // 2
    piece = pieces.shape[1] - 16
    total = ins[0][: 2 * n, :].astype(F32)
    bias = ins[0][2 * n :, :n].astype(F32)
    for part in ins[1:]:
        total = total + part[: 2 * n, :].astype(F32)
        bias = bias + part[2 * n :, :n].astype(F32)
    turned = total.T.astype(BF)
    bias = jnp.sum(bias, axis=0, keepdims=True)
    for c in range(SIDE):
        pieces[c, :piece, :] = turned[c * piece : (c + 1) * piece]
        shifted = pltpu.roll(bias, (n - c * (n // (SIDE * SIDE))) % n, 1)
        pieces[c, piece:, :n] = hi_lo(shifted)
        pieces[c, piece:, n:] = jnp.zeros((16, n), BF)
    hand_out(pieces, outs, lax.rem(lax.axis_index("rows"), SIDE), sems)


def first_sum(parts):
    rows, quarter = parts[0].shape
    piece = (quarter // SIDE + 16, rows - 16)
    return pl.pallas_call(
        first_sum_kernel,
        out_shape=[jax.ShapeDtypeStruct(piece, BF)] * SIDE,
        out_specs=[pl.BlockSpec(memory_space=pl.ANY)] * SIDE,
        scratch_shapes=[pltpu.VMEM((SIDE,) + piece, BF), pltpu.SemaphoreType.DMA((SIDE,))],
        compiler_params=PARAMS,
        name="sum_over_y",
    )(*parts)


def last_sum_kernel(*refs):
    ins, (enc_ref, dec_ref, bias_ref) = refs[:SIDE], refs[SIDE:]
    rows, cols = ins[0].shape
    piece, n = rows - 16, cols // 2
    total = ins[0][...].astype(F32)
    for part in ins[1:]:
        total = total + part[...].astype(F32)
    enc_ref[...] = total[:piece, :n]
    dec_ref[...] = total[:piece, n:]
    bias = jnp.sum(total[piece:, :n], axis=0, keepdims=True)
    bias_ref[...] = bias[:, : bias_ref.shape[1]]


def last_sum(parts, own):
    rows, cols = parts[0].shape
    piece, n = rows - 16, cols // 2
    return pl.pallas_call(
        last_sum_kernel,
        out_shape=[
            jax.ShapeDtypeStruct((piece, n), F32),
            jax.ShapeDtypeStruct((piece, n), F32),
            jax.ShapeDtypeStruct((1, own), F32),
        ],
        compiler_params=PARAMS,
        name="sum_over_z",
    )(*parts)


def share_pieces(pieces, along_y):
    got = [pieces[0]]
    for k in (1, 3, 2):
        pairs = []
        for i in range(SIDE * SIDE):
            y, z = divmod(i, SIDE)
            to = ((y + k) % SIDE, z) if along_y else (y, (z + k) % SIDE)
            pairs.append((i, to[0] * SIDE + to[1]))
        got.append(lax.ppermute(pieces[k], "rows", pairs))
    return got


def along_z(x, step):
    if step == 0:
        return x
    pairs = []
    for i in range(512):
        rows, lat = divmod(i, 32)
        y, z_hi = divmod(rows, SIDE)
        x_place, rest = divmod(lat, 2 * SIDE)
        z_lo, core = divmod(rest, 2)
        z = (z_hi * SIDE + z_lo + step) % (SIDE * SIDE)
        to_rows = y * SIDE + z // SIDE
        pairs.append((i, to_rows * 32 + x_place * 2 * SIDE + z % SIDE * 2 + core))
    return lax.ppermute(x, ("rows", "lat"), pairs)


def over_x(x):
    groups = [
        [xp * 2 * SIDE + z * 2 + core for xp in range(SIDE) for core in range(2)]
        for z in range(SIDE)
    ]
    members = 2 * SIDE
    shape = x.shape
    out = lax.all_to_all(
        x.reshape(members, shape[0] // members, shape[1]),
        "lat",
        split_axis=0,
        concat_axis=0,
        axis_index_groups=groups,
        tiled=True,
    )
    return out.reshape(shape)


def to_owners(slots):
    moved = [along_z(a, step) for a, step in zip(slots[:5], STEPS)]
    crossed, merged = lax.optimization_barrier((over_x(slots[5]), swap_pieces(moved, True)))
    stream_a = over_x(merged)
    stream_b = [along_z(a, step) for a, step in zip(swap_pieces([crossed], False), STEPS)]
    return stream_a, stream_b


def to_homes(stream_a, stream_b):
    moved = [along_z(a, -step) for a, step in zip(stream_b, STEPS)]
    crossed, merged = lax.optimization_barrier((over_x(stream_a), swap_pieces(moved, True)))
    home_b = over_x(merged)
    home_a = [along_z(a, -step) for a, step in zip(swap_pieces([crossed], False), STEPS)]
    return [*home_a, home_b]


def local(activations, block_ids, enc_weight, enc_bias, dec_weight, dec_bias):
    blocks = lax.axis_size("lat")
    parts_rows = lax.axis_size("rows")
    n = enc_weight.shape[1]
    ids = block_ids.T
    bias = enc_bias[None, :]
    x_a, x_b = to_owners(pack(ids, activations, blocks))
    dec_a, pre_a = encode_decode([x_a], enc_weight, bias, dec_weight)
    x_b, dec_a = lax.optimization_barrier((x_b, dec_a))
    *dec_b, pre_b = encode_decode(x_b, enc_weight, bias, dec_weight)
    back = to_homes(dec_a, dec_b)
    e_a, e_b = to_owners(error_rows(ids, back, activations, dec_bias[None, :], blocks))
    terms = gradients([*x_b, x_a], [*e_b, e_a], pre_a, pre_b, dec_weight)
    terms = share_pieces(terms, True)
    terms = share_pieces(first_sum(terms), False)
    enc_grad, dec_turned, bias_grad = last_sum(terms, n // parts_rows)
    return enc_grad, dec_turned.T, bias_grad.reshape(-1)


def solution(mesh):
    in_specs = (
        P(("rows", "lat"), None),
        P(("rows", "lat"), None),
        P(None, "lat"),
        P("lat"),
        P("lat", None),
        P(),
    )
    out_specs = (P("rows", "lat"), P("lat", "rows"), P(("lat", "rows")))
    return jax.shard_map(local, mesh=mesh, in_specs=in_specs, out_specs=out_specs, check_vma=False)
```

```python
import functools

import jax
import jax.numpy as jnp
from jax import lax
from jax.experimental import pallas as pl
from jax.experimental.pallas import tpu as pltpu
from jax.sharding import PartitionSpec as P

SLOTS = 6
PAIR = 2 * SLOTS
SIDE = 4
STEPS = ((0, 0), (1, 1), (2, -2), (-1, -1))
BF = jnp.bfloat16
F32 = jnp.float32
VMEM = 56 * 1024 * 1024
COLS = 256
PARAMS = pltpu.CompilerParams(vmem_limit_bytes=VMEM)
ANY = pl.BlockSpec(memory_space=pl.ANY)


def by_twelve(row):
    return lax.shift_right_logical(row * 5462, 16)


def dot(a, b):
    return lax.dot_general(a, b, (((1,), (0,)), ((), ())), preferred_element_type=F32)


def dot_t(a, b):
    return lax.dot_general(a, b, (((0,), (0,)), ((), ())), preferred_element_type=F32)


def dot_nt(a, b):
    return lax.dot_general(a, b, (((1,), (1,)), ((), ())), preferred_element_type=F32)


def left_rows(rows):
    row = lax.broadcasted_iota(jnp.int32, (rows, 1), 0)
    return row - by_twelve(row) * PAIR < SLOTS


def split_halves(x, left):
    zero = jnp.zeros_like(x)
    return jnp.concatenate([jnp.where(left, x, zero), jnp.where(left, zero, x)], axis=1)


def join_halves(y, left):
    rows, n = y.shape[0], y.shape[1] // 2
    yl, yr = y[:, :n], y[:, n:]
    after = pltpu.roll(yr, rows - SLOTS, 0)
    before = pltpu.roll(yl, SLOTS, 0)
    return jnp.where(left, yl + after, yr + before)


def one_hot_slots(ids, blocks):
    n = ids.shape[1]
    rows = 2 * blocks * PAIR
    number = lax.broadcasted_iota(jnp.int32, (blocks, n), 0)
    member = (number == ids[0:1, :]) | (number == ids[1:2, :])
    earlier = (
        lax.broadcasted_iota(jnp.int32, (n, n), 0) < lax.broadcasted_iota(jnp.int32, (n, n), 1)
    )
    position = dot(member.astype(F32).astype(BF), earlier.astype(F32).astype(BF))
    code = jnp.where(member, position, 200.0).astype(BF)
    zl = lax.rem(lax.axis_index("lat") // 2, SIDE)
    row = lax.broadcasted_iota(jnp.int32, (rows, 1), 0)
    piece = by_twelve(row)
    place = row - piece * PAIR
    first = piece < blocks
    in_a, in_b = piece, piece - blocks
    xc = jnp.where(first, in_a & 7, lax.shift_right_logical(in_b, 2))
    k = jnp.where(first, lax.shift_right_logical(in_a, 3), in_b & 3)
    block = lax.shift_right_logical(xc, 1) * (2 * SIDE) + ((zl + k) & 3) * 2 + (xc & 1)
    left = place < SLOTS
    slot = place - jnp.where(left, 0, SLOTS) + jnp.where(first, 0, SLOTS)
    expand = lax.broadcasted_iota(jnp.int32, (rows, blocks), 1) == block
    spread = dot(expand.astype(F32).astype(BF), code)
    hit = (spread == slot.astype(F32)).astype(F32)
    return split_halves(hit, left).astype(BF)


def start(pairs, sems, first=0):
    copies = [pltpu.make_async_copy(a, b, sems.at[first + i]) for i, (a, b) in enumerate(pairs)]
    for copy in copies:
        copy.start()
    return copies


def wait(copies):
    for copy in copies:
        copy.wait()


def send_slots(sel, rows2, slots, outs, sems):
    total, half = slots.shape
    rows = total // 2
    part = rows // SIDE
    copies = []
    for i in range(2):
        own = slice(i * rows, (i + 1) * rows)
        chosen = sel[own, :]
        for c in range(0, half, COLS):
            slots[own, c : c + COLS] = dot(chosen, rows2[:, c : c + COLS]).astype(BF)
        if i == 0:
            copies += start(
                [(slots.at[k * part : (k + 1) * part], outs[k]) for k in range(SIDE)], sems
            )
        else:
            copies += start([(slots.at[rows:], outs[SIDE])], sems, SIDE)
    wait(copies)


def slot_shapes(blocks, half):
    total = blocks * PAIR
    part = total // SIDE
    shapes = [jax.ShapeDtypeStruct((part, half), BF)] * SIDE
    return shapes + [jax.ShapeDtypeStruct((total, half), BF)]


def pack_kernel(blocks, ids_ref, act_ref, *refs):
    outs, (act2, sel, pieces, in_sems, sems) = refs[: SIDE + 1], refs[SIDE + 1 :]
    n, width = act_ref.shape
    half = width // 2
    copies = start(
        [(act_ref.at[:, s * half : (s + 1) * half], act2.at[s * n : (s + 1) * n]) for s in range(2)],
        in_sems,
    )
    sel[...] = one_hot_slots(ids_ref[...], blocks)
    wait(copies)
    send_slots(sel, act2, pieces, outs, sems)


def pack(ids, act, blocks):
    n, width = act.shape
    half = width // 2
    part = blocks * PAIR // SIDE
    return pl.pallas_call(
        functools.partial(pack_kernel, blocks),
        in_specs=[pl.BlockSpec(memory_space=pltpu.VMEM), ANY],
        out_specs=[ANY] * (SIDE + 1),
        out_shape=slot_shapes(blocks, half),
        scratch_shapes=[
            pltpu.VMEM((2 * n, half), BF),
            pltpu.VMEM((2 * SIDE * part, 2 * n), BF),
            pltpu.VMEM((2 * SIDE * part, half), BF),
            pltpu.SemaphoreType.DMA((2,)),
            pltpu.SemaphoreType.DMA((SIDE + 1,)),
        ],
        compiler_params=PARAMS,
        name="pack_rows",
    )(ids, act)


def swap_kernel(merge, *refs):
    if merge:
        ins, out_ref, (pieces, done, in_sems, sems) = refs[:SIDE], refs[SIDE], refs[SIDE + 1 :]
    else:
        in_ref, outs, (pieces, done, in_sems, sems) = refs[0], refs[1 : SIDE + 1], refs[SIDE + 1 :]
    rows = pieces.shape[1]
    part = rows // SIDE
    halves = range(2)
    if merge:
        moves = [
            [
                (ins[k].at[h * part : (h + 1) * part], pieces.at[h, k * part : (k + 1) * part])
                for k in range(SIDE)
            ]
            for h in halves
        ]
    else:
        moves = [[(in_ref.at[h * rows : (h + 1) * rows], pieces.at[h])] for h in halves]
    copies = [start(moves[h], in_sems, h * SIDE) for h in halves]
    row = lax.broadcasted_iota(jnp.int32, (rows, 1), 0)
    piece = by_twelve(row)
    source = (piece & 3) * part + lax.shift_right_logical(piece, 2) * PAIR + row - piece * PAIR
    turn = (lax.broadcasted_iota(jnp.int32, (rows, rows), 1) == source).astype(F32).astype(BF)
    sent = []
    for h in halves:
        wait(copies[h])
        done[h] = dot(turn, pieces[h]).astype(BF)
        if merge:
            sent += start([(done.at[h], out_ref.at[h * rows : (h + 1) * rows])], sems, h * SIDE)
        else:
            sent += start(
                [
                    (done.at[h, k * part : (k + 1) * part], outs[k].at[h * part : (h + 1) * part])
                    for k in range(SIDE)
                ],
                sems,
                h * SIDE,
            )
    wait(sent)


def swap_pieces(arrays, merge):
    total = arrays[0].shape[0] * (SIDE if merge else 1)
    half = arrays[0].shape[1]
    shape = jax.ShapeDtypeStruct((total, half), BF)
    shapes = [jax.ShapeDtypeStruct((total // SIDE, half), BF)] * SIDE
    return pl.pallas_call(
        functools.partial(swap_kernel, merge),
        in_specs=[ANY] * len(arrays),
        out_specs=ANY if merge else [ANY] * SIDE,
        out_shape=shape if merge else shapes,
        scratch_shapes=[
            pltpu.VMEM((2, total // 2, half), BF),
            pltpu.VMEM((2, total // 2, half), BF),
            pltpu.SemaphoreType.DMA((2 * SIDE,)),
            pltpu.SemaphoreType.DMA((2 * SIDE,)),
        ],
        compiler_params=PARAMS,
        name="merge_pieces" if merge else "split_pieces",
    )(*arrays)


def code_kernel(parts, *refs):
    ins, (enc_ref, bias_ref, dec_ref) = refs[:parts], refs[parts : parts + 3]
    outs, pre_ref = refs[parts + 3 : 2 * parts + 3], refs[2 * parts + 3]
    enc2, dec2, x, done, w_sems, in_sems, sems = refs[2 * parts + 4 :]
    half, n = enc2.shape[0], enc2.shape[1] // 2
    total = x.shape[0]
    rows = total // parts

    def moves(refs, buffer):
        return [(refs[i], buffer.at[i * rows : (i + 1) * rows]) for i in range(parts)]

    enc_copies = start(
        [(enc_ref.at[s * half : (s + 1) * half], enc2.at[:, s * n : (s + 1) * n]) for s in range(2)],
        w_sems,
    )
    in_copies = start(moves(ins, x), in_sems)
    dec_copies = start(
        [(dec_ref.at[:, s * half : (s + 1) * half], dec2.at[s * n : (s + 1) * n]) for s in range(2)],
        w_sems,
        2,
    )
    left = left_rows(total)
    wait(enc_copies)
    wait(in_copies)
    pre = join_halves(dot(x[...], enc2[...]), left) + bias_ref[...]
    pre_ref[...] = pre
    codes = split_halves(pre * jax.nn.sigmoid(pre), left).astype(BF)
    wait(dec_copies)
    for c in range(0, half, COLS):
        done[:, c : c + COLS] = dot(codes, dec2[:, c : c + COLS]).astype(BF)
    wait(start([(b, a) for a, b in moves(outs, done)], sems))


def encode_decode(x, enc, bias, dec):
    width, n = enc.shape
    half = width // 2
    parts = len(x)
    total = sum(a.shape[0] for a in x)
    return pl.pallas_call(
        functools.partial(code_kernel, parts),
        in_specs=[ANY] * (parts + 1) + [pl.BlockSpec(memory_space=pltpu.VMEM), ANY],
        out_specs=[ANY] * parts + [pl.BlockSpec(memory_space=pltpu.VMEM)],
        out_shape=[jax.ShapeDtypeStruct(a.shape, BF) for a in x]
        + [jax.ShapeDtypeStruct((total, n), F32)],
        scratch_shapes=[
            pltpu.VMEM((half, 2 * n), BF),
            pltpu.VMEM((2 * n, half), BF),
            pltpu.VMEM((total, half), BF),
            pltpu.VMEM((total, half), BF),
            pltpu.SemaphoreType.DMA((4,)),
            pltpu.SemaphoreType.DMA((SIDE,)),
            pltpu.SemaphoreType.DMA((SIDE,)),
        ],
        compiler_params=PARAMS,
        name="encode_decode",
    )(*x, enc, bias, dec)


def slot_moves(refs, buffer):
    part = refs[0].shape[0]
    pairs = [(refs[k], buffer.at[k * part : (k + 1) * part]) for k in range(SIDE)]
    return pairs + [(refs[SIDE], buffer.at[SIDE * part :])]


def error_kernel(blocks, ids_ref, bias_ref, act_ref, *refs):
    ins, outs = refs[: SIDE + 1], refs[SIDE + 1 : 2 * SIDE + 2]
    act2, back, sel, err2, pieces, act_sems, in_sems, sems = refs[2 * SIDE + 2 :]
    n, width = act_ref.shape
    half = width // 2
    copies = start(slot_moves(ins, back), in_sems)
    copies += start(
        [(act_ref.at[:, s * half : (s + 1) * half], act2.at[s * n : (s + 1) * n]) for s in range(2)],
        act_sems,
    )
    sel[...] = one_hot_slots(ids_ref[...], blocks)
    wait(copies)
    step = COLS
    for c in range(0, half, step):
        sums = dot_t(sel[...], back[:, c : c + step])
        for s in range(2):
            rows = slice(s * n, (s + 1) * n)
            bias = bias_ref[:, s * half + c : s * half + c + step]
            wanted = act2[rows, c : c + step].astype(F32)
            err2[rows, c : c + step] = ((sums[rows] + bias - wanted) * (1.0 / 64.0)).astype(BF)
    send_slots(sel, err2, pieces, outs, sems)


def error_rows(ids, back, act, bias, blocks):
    n, width = act.shape
    half = width // 2
    total = 2 * blocks * PAIR
    in_vmem = pl.BlockSpec(memory_space=pltpu.VMEM)
    return pl.pallas_call(
        functools.partial(error_kernel, blocks),
        in_specs=[in_vmem, in_vmem] + [ANY] * (SIDE + 2),
        out_specs=[ANY] * (SIDE + 1),
        out_shape=slot_shapes(blocks, half),
        scratch_shapes=[
            pltpu.VMEM((2 * n, half), BF),
            pltpu.VMEM((total, half), BF),
            pltpu.VMEM((total, 2 * n), BF),
            pltpu.VMEM((2 * n, half), BF),
            pltpu.VMEM((total, half), BF),
            pltpu.SemaphoreType.DMA((2,)),
            pltpu.SemaphoreType.DMA((SIDE + 1,)),
            pltpu.SemaphoreType.DMA((SIDE + 1,)),
        ],
        compiler_params=PARAMS,
        name="error_rows",
    )(ids, bias, act, *back)


def hi_lo(x):
    hi = x.astype(BF).astype(F32)
    row = lax.broadcasted_iota(jnp.int32, (16, x.shape[1]), 0)
    return jnp.where(row == 0, hi, jnp.where(row == 1, x - hi, 0.0)).astype(BF)


def grad_kernel(pre_a, pre_b, dec_ref, *refs):
    x_refs, e_refs, outs = refs[: SIDE + 1], refs[SIDE + 1 : 2 * SIDE + 2], refs[2 * SIDE + 2 : 3 * SIDE + 2]
    dec2, x, e, pieces, w_sems, x_sems, e_sems, sems = refs[3 * SIDE + 2 :]
    rows, half = x.shape
    n = pre_a.shape[1]
    groups, _, quarter = pieces.shape
    dec_copies = start(
        [(dec_ref.at[:, s * half : (s + 1) * half], dec2.at[s * n : (s + 1) * n]) for s in range(2)],
        w_sems,
    )
    e_copies = start(slot_moves(e_refs, e), e_sems)
    x_copies = start(slot_moves(x_refs, x), x_sems)
    me = lax.axis_index("rows") // SIDE
    left = left_rows(rows)
    pre = jnp.concatenate([pre_b[...], pre_a[...]], axis=0)
    sig = jax.nn.sigmoid(pre)
    codes = split_halves(pre * sig, left).astype(BF)
    wait(dec_copies)
    wait(e_copies)
    code_grad = join_halves(dot_nt(e[...], dec2[...]), left)
    grad = (code_grad * sig * (1.0 + pre * (1.0 - sig))).astype(BF).astype(F32)
    grads = split_halves(grad, left)
    bias = jnp.sum(grads[:, :n], axis=0, keepdims=True)
    grads = grads.astype(BF)
    wait(x_copies)
    for g in range(0, groups // 2):
        cols = pl.ds(g * quarter, quarter)
        enc = dot_t(grads, x[:, cols]).astype(BF)
        dec = dot_t(codes, e[:, cols]).astype(BF)
        for s in range(2):
            pieces[g + s * (groups // 2), :n, :] = enc[s * n : s * n + n]
            pieces[g + s * (groups // 2), n : 2 * n, :] = dec[s * n : s * n + n]
    for g in range(groups):
        shifted = pltpu.roll(bias, (n - g * (n // groups)) % n, 1)
        pieces[g, 2 * n :, :] = jnp.zeros((16, quarter), BF)
        pieces[g, 2 * n :, :n] = hi_lo(shifted)
    hand_out(pieces, outs, me, sems)


def hand_out(pieces, outs, me, sems):
    wait(start([(pieces.at[lax.rem(me + k, SIDE)], out) for k, out in enumerate(outs)], sems))


def gradients(x, err, pre_a, pre_b, dec):
    n, width = dec.shape
    piece = (2 * n + 16, width // SIDE)
    rows = 2 * pre_a.shape[0]
    in_vmem = pl.BlockSpec(memory_space=pltpu.VMEM)
    return pl.pallas_call(
        grad_kernel,
        in_specs=[in_vmem, in_vmem] + [ANY] * (2 * SIDE + 3),
        out_shape=[jax.ShapeDtypeStruct(piece, BF)] * SIDE,
        out_specs=[ANY] * SIDE,
        scratch_shapes=[
            pltpu.VMEM((2 * n, width // 2), BF),
            pltpu.VMEM((rows, width // 2), BF),
            pltpu.VMEM((rows, width // 2), BF),
            pltpu.VMEM((SIDE,) + piece, BF),
            pltpu.SemaphoreType.DMA((2,)),
            pltpu.SemaphoreType.DMA((SIDE + 1,)),
            pltpu.SemaphoreType.DMA((SIDE + 1,)),
            pltpu.SemaphoreType.DMA((SIDE,)),
        ],
        compiler_params=PARAMS,
        name="gradients",
    )(pre_a, pre_b, dec, *x, *err)


def first_sum_kernel(*refs):
    ins, outs, (pieces, sems) = refs[:SIDE], refs[SIDE : 2 * SIDE], refs[2 * SIDE :]
    rows, quarter = ins[0].shape
    n = (rows - 16) // 2
    piece = pieces.shape[1] - 16
    total = ins[0][: 2 * n, :].astype(F32)
    bias = ins[0][2 * n :, :n].astype(F32)
    for part in ins[1:]:
        total = total + part[: 2 * n, :].astype(F32)
        bias = bias + part[2 * n :, :n].astype(F32)
    turned = total.T.astype(BF)
    bias = jnp.sum(bias, axis=0, keepdims=True)
    for c in range(SIDE):
        pieces[c, :piece, :] = turned[c * piece : (c + 1) * piece]
        shifted = pltpu.roll(bias, (n - c * (n // (SIDE * SIDE))) % n, 1)
        pieces[c, piece:, :n] = hi_lo(shifted)
        pieces[c, piece:, n:] = jnp.zeros((16, n), BF)
    hand_out(pieces, outs, lax.rem(lax.axis_index("rows"), SIDE), sems)


def first_sum(parts):
    rows, quarter = parts[0].shape
    piece = (quarter // SIDE + 16, rows - 16)
    return pl.pallas_call(
        first_sum_kernel,
        out_shape=[jax.ShapeDtypeStruct(piece, BF)] * SIDE,
        out_specs=[pl.BlockSpec(memory_space=pl.ANY)] * SIDE,
        scratch_shapes=[pltpu.VMEM((SIDE,) + piece, BF), pltpu.SemaphoreType.DMA((SIDE,))],
        compiler_params=PARAMS,
        name="sum_over_y",
    )(*parts)


def last_sum_kernel(*refs):
    ins, (enc_ref, dec_ref, bias_ref) = refs[:SIDE], refs[SIDE:]
    rows, cols = ins[0].shape
    piece, n = rows - 16, cols // 2
    total = ins[0][...].astype(F32)
    for part in ins[1:]:
        total = total + part[...].astype(F32)
    enc_ref[...] = total[:piece, :n]
    dec_ref[...] = total[:piece, n:]
    bias = jnp.sum(total[piece:, :n], axis=0, keepdims=True)
    bias_ref[...] = bias[:, : bias_ref.shape[1]]


def last_sum(parts, own):
    rows, cols = parts[0].shape
    piece, n = rows - 16, cols // 2
    return pl.pallas_call(
        last_sum_kernel,
        out_shape=[
            jax.ShapeDtypeStruct((piece, n), F32),
            jax.ShapeDtypeStruct((piece, n), F32),
            jax.ShapeDtypeStruct((1, own), F32),
        ],
        compiler_params=PARAMS,
        name="sum_over_z",
    )(*parts)


def share_pieces(pieces, along_y):
    got = [pieces[0]]
    for k in (1, 3, 2):
        pairs = []
        for i in range(SIDE * SIDE):
            y, z = divmod(i, SIDE)
            to = ((y + k) % SIDE, z) if along_y else (y, (z + k) % SIDE)
            pairs.append((i, to[0] * SIDE + to[1]))
        got.append(lax.ppermute(pieces[k], "rows", pairs))
    return got


def along_z(x, steps, back=False):
    if steps[0] == 0:
        return x
    pairs = []
    for i in range(512):
        rows, lat = divmod(i, 32)
        y, z_hi = divmod(rows, SIDE)
        x_place, rest = divmod(lat, 2 * SIDE)
        z_lo, core = divmod(rest, 2)
        step = -steps[core] if back else steps[core]
        z = (z_hi * SIDE + z_lo + step) % (SIDE * SIDE)
        to_rows = y * SIDE + z // SIDE
        pairs.append((i, to_rows * 32 + x_place * 2 * SIDE + z % SIDE * 2 + core))
    return lax.ppermute(x, ("rows", "lat"), pairs)


def over_x(x):
    groups = [
        [xp * 2 * SIDE + z * 2 + core for xp in range(SIDE) for core in range(2)]
        for z in range(SIDE)
    ]
    members = 2 * SIDE
    shape = x.shape
    out = lax.all_to_all(
        x.reshape(members, shape[0] // members, shape[1]),
        "lat",
        split_axis=0,
        concat_axis=0,
        axis_index_groups=groups,
        tiled=True,
    )
    return out.reshape(shape)


def to_owners(slots):
    moved = [along_z(a, steps) for a, steps in zip(slots[:SIDE], STEPS)]
    crossed, merged = lax.optimization_barrier((over_x(slots[SIDE]), swap_pieces(moved, True)))
    stream_a = over_x(merged)
    stream_b = [along_z(a, steps) for a, steps in zip(swap_pieces([crossed], False), STEPS)]
    return stream_a, stream_b


def to_homes(stream_a, stream_b):
    moved = [along_z(a, steps, True) for a, steps in zip(stream_b, STEPS)]
    crossed, merged = lax.optimization_barrier((over_x(stream_a), swap_pieces(moved, True)))
    home_b = over_x(merged)
    home_a = [along_z(a, steps, True) for a, steps in zip(swap_pieces([crossed], False), STEPS)]
    return [*home_a, home_b]


def local(activations, block_ids, enc_weight, enc_bias, dec_weight, dec_bias):
    blocks = lax.axis_size("lat")
    parts_rows = lax.axis_size("rows")
    n = enc_weight.shape[1]
    ids = block_ids.T
    bias = enc_bias[None, :]
    x_a, x_b = to_owners(pack(ids, activations, blocks))
    dec_a, pre_a = encode_decode([x_a], enc_weight, bias, dec_weight)
    x_b, dec_a = lax.optimization_barrier((x_b, dec_a))
    *dec_b, pre_b = encode_decode(x_b, enc_weight, bias, dec_weight)
    back = to_homes(dec_a, dec_b)
    e_a, e_b = to_owners(error_rows(ids, back, activations, dec_bias[None, :], blocks))
    terms = gradients([*x_b, x_a], [*e_b, e_a], pre_a, pre_b, dec_weight)
    terms = share_pieces(terms, True)
    terms = share_pieces(first_sum(terms), False)
    enc_grad, dec_turned, bias_grad = last_sum(terms, n // parts_rows)
    return enc_grad, dec_turned.T, bias_grad.reshape(-1)


def solution(mesh):
    in_specs = (
        P(("rows", "lat"), None),
        P(("rows", "lat"), None),
        P(None, "lat"),
        P("lat"),
        P("lat", None),
        P(),
    )
    out_specs = (P("rows", "lat"), P("lat", "rows"), P(("lat", "rows")))
    return jax.shard_map(local, mesh=mesh, in_specs=in_specs, out_specs=out_specs, check_vma=False)
```

```python
import functools

import jax
import jax.numpy as jnp
from jax import lax
from jax.experimental import pallas as pl
from jax.experimental.pallas import tpu as pltpu
from jax.sharding import PartitionSpec as P

SLOTS = 6
PAIR = 2 * SLOTS
SIDE = 4
STEPS = ((0, 0), (1, 1), (2, -2), (-1, -1))
BF = jnp.bfloat16
F32 = jnp.float32
VMEM = 56 * 1024 * 1024
COLS = 256
PARAMS = pltpu.CompilerParams(vmem_limit_bytes=VMEM)
ANY = pl.BlockSpec(memory_space=pl.ANY)


def by_twelve(row):
    return lax.shift_right_logical(row * 5462, 16)


def dot(a, b):
    return lax.dot_general(a, b, (((1,), (0,)), ((), ())), preferred_element_type=F32)


def dot_t(a, b):
    return lax.dot_general(a, b, (((0,), (0,)), ((), ())), preferred_element_type=F32)


def dot_nt(a, b):
    return lax.dot_general(a, b, (((1,), (1,)), ((), ())), preferred_element_type=F32)


def left_rows(rows):
    row = lax.broadcasted_iota(jnp.int32, (rows, 1), 0)
    return row - by_twelve(row) * PAIR < SLOTS


def split_halves(x, left):
    zero = jnp.zeros_like(x)
    return jnp.concatenate([jnp.where(left, x, zero), jnp.where(left, zero, x)], axis=1)


def join_halves(y, left):
    rows, n = y.shape[0], y.shape[1] // 2
    yl, yr = y[:, :n], y[:, n:]
    after = pltpu.roll(yr, rows - SLOTS, 0)
    before = pltpu.roll(yl, SLOTS, 0)
    return jnp.where(left, yl + after, yr + before)


def one_hot_slots(ids, blocks):
    n = ids.shape[1]
    rows = 2 * blocks * PAIR
    number = lax.broadcasted_iota(jnp.int32, (blocks, n), 0)
    member = (number == ids[0:1, :]) | (number == ids[1:2, :])
    earlier = (
        lax.broadcasted_iota(jnp.int32, (n, n), 0) < lax.broadcasted_iota(jnp.int32, (n, n), 1)
    )
    position = dot(member.astype(F32).astype(BF), earlier.astype(F32).astype(BF))
    code = jnp.where(member, position, 200.0).astype(BF)
    zl = lax.rem(lax.axis_index("lat") // 2, SIDE)
    row = lax.broadcasted_iota(jnp.int32, (rows, 1), 0)
    piece = by_twelve(row)
    place = row - piece * PAIR
    first = piece < blocks
    in_a, in_b = piece, piece - blocks
    xc = jnp.where(first, in_a & 7, lax.shift_right_logical(in_b, 2))
    k = jnp.where(first, lax.shift_right_logical(in_a, 3), in_b & 3)
    block = lax.shift_right_logical(xc, 1) * (2 * SIDE) + ((zl + k) & 3) * 2 + (xc & 1)
    left = place < SLOTS
    slot = place - jnp.where(left, 0, SLOTS) + jnp.where(first, 0, SLOTS)
    expand = lax.broadcasted_iota(jnp.int32, (rows, blocks), 1) == block
    spread = dot(expand.astype(F32).astype(BF), code)
    hit = (spread == slot.astype(F32)).astype(F32)
    return split_halves(hit, left).astype(BF)


def start(pairs, sems, first=0):
    copies = [pltpu.make_async_copy(a, b, sems.at[first + i]) for i, (a, b) in enumerate(pairs)]
    for copy in copies:
        copy.start()
    return copies


def wait(copies):
    for copy in copies:
        copy.wait()


def send_slots(sel, rows2, slots, outs, sems):
    total, half = slots.shape
    rows = total // 2
    part = rows // SIDE
    copies = []
    for i in range(2):
        own = slice(i * rows, (i + 1) * rows)
        chosen = sel[own, :]
        for c in range(0, half, COLS):
            slots[own, c : c + COLS] = dot(chosen, rows2[:, c : c + COLS]).astype(BF)
        if i == 0:
            copies += start(
                [(slots.at[k * part : (k + 1) * part], outs[k]) for k in range(SIDE)], sems
            )
        else:
            copies += start([(slots.at[rows:], outs[SIDE])], sems, SIDE)
    wait(copies)


def slot_shapes(blocks, half):
    total = blocks * PAIR
    part = total // SIDE
    shapes = [jax.ShapeDtypeStruct((part, half), BF)] * SIDE
    return shapes + [jax.ShapeDtypeStruct((total, half), BF)]


def pack_kernel(blocks, ids_ref, act_ref, *refs):
    outs, (act2, sel, pieces, in_sems, sems) = refs[: SIDE + 1], refs[SIDE + 1 :]
    n, width = act_ref.shape
    half = width // 2
    copies = start(
        [(act_ref.at[:, s * half : (s + 1) * half], act2.at[s * n : (s + 1) * n]) for s in range(2)],
        in_sems,
    )
    sel[...] = one_hot_slots(ids_ref[...], blocks)
    wait(copies)
    send_slots(sel, act2, pieces, outs, sems)


def pack(ids, act, blocks):
    n, width = act.shape
    half = width // 2
    part = blocks * PAIR // SIDE
    return pl.pallas_call(
        functools.partial(pack_kernel, blocks),
        in_specs=[pl.BlockSpec(memory_space=pltpu.VMEM), ANY],
        out_specs=[ANY] * (SIDE + 1),
        out_shape=slot_shapes(blocks, half),
        scratch_shapes=[
            pltpu.VMEM((2 * n, half), BF),
            pltpu.VMEM((2 * SIDE * part, 2 * n), BF),
            pltpu.VMEM((2 * SIDE * part, half), BF),
            pltpu.SemaphoreType.DMA((2,)),
            pltpu.SemaphoreType.DMA((SIDE + 1,)),
        ],
        compiler_params=PARAMS,
        name="pack_rows",
    )(ids, act)


def swap_kernel(merge, *refs):
    if merge:
        ins, out_ref, (pieces, done, in_sems, sems) = refs[:SIDE], refs[SIDE], refs[SIDE + 1 :]
    else:
        in_ref, outs, (pieces, done, in_sems, sems) = refs[0], refs[1 : SIDE + 1], refs[SIDE + 1 :]
    rows = pieces.shape[1]
    part = rows // SIDE
    halves = range(2)
    if merge:
        moves = [
            [
                (ins[k].at[h * part : (h + 1) * part], pieces.at[h, k * part : (k + 1) * part])
                for k in range(SIDE)
            ]
            for h in halves
        ]
    else:
        moves = [[(in_ref.at[h * rows : (h + 1) * rows], pieces.at[h])] for h in halves]
    copies = [start(moves[h], in_sems, h * SIDE) for h in halves]
    row = lax.broadcasted_iota(jnp.int32, (rows, 1), 0)
    piece = by_twelve(row)
    source = (piece & 3) * part + lax.shift_right_logical(piece, 2) * PAIR + row - piece * PAIR
    turn = (lax.broadcasted_iota(jnp.int32, (rows, rows), 1) == source).astype(F32).astype(BF)
    sent = []
    for h in halves:
        wait(copies[h])
        done[h] = dot(turn, pieces[h]).astype(BF)
        if merge:
            sent += start([(done.at[h], out_ref.at[h * rows : (h + 1) * rows])], sems, h * SIDE)
        else:
            sent += start(
                [
                    (done.at[h, k * part : (k + 1) * part], outs[k].at[h * part : (h + 1) * part])
                    for k in range(SIDE)
                ],
                sems,
                h * SIDE,
            )
    wait(sent)


def swap_pieces(arrays, merge):
    total = arrays[0].shape[0] * (SIDE if merge else 1)
    half = arrays[0].shape[1]
    shape = jax.ShapeDtypeStruct((total, half), BF)
    shapes = [jax.ShapeDtypeStruct((total // SIDE, half), BF)] * SIDE
    return pl.pallas_call(
        functools.partial(swap_kernel, merge),
        in_specs=[ANY] * len(arrays),
        out_specs=ANY if merge else [ANY] * SIDE,
        out_shape=shape if merge else shapes,
        scratch_shapes=[
            pltpu.VMEM((2, total // 2, half), BF),
            pltpu.VMEM((2, total // 2, half), BF),
            pltpu.SemaphoreType.DMA((2 * SIDE,)),
            pltpu.SemaphoreType.DMA((2 * SIDE,)),
        ],
        compiler_params=PARAMS,
        name="merge_pieces" if merge else "split_pieces",
    )(*arrays)


def code_kernel(parts, *refs):
    ins, (enc_ref, bias_ref, dec_ref) = refs[:parts], refs[parts : parts + 3]
    outs, pre_ref = refs[parts + 3 : 2 * parts + 3], refs[2 * parts + 3]
    enc2, dec2, x, done, w_sems, in_sems, sems = refs[2 * parts + 4 :]
    half, n = enc2.shape[0], enc2.shape[1] // 2
    total = x.shape[0]
    rows = total // parts

    def moves(refs, buffer):
        return [(refs[i], buffer.at[i * rows : (i + 1) * rows]) for i in range(parts)]

    enc_copies = start(
        [(enc_ref.at[s * half : (s + 1) * half], enc2.at[:, s * n : (s + 1) * n]) for s in range(2)],
        w_sems,
    )
    in_copies = start(moves(ins, x), in_sems)
    dec_copies = start(
        [(dec_ref.at[:, s * half : (s + 1) * half], dec2.at[s * n : (s + 1) * n]) for s in range(2)],
        w_sems,
        2,
    )
    left = left_rows(total)
    wait(enc_copies)
    wait(in_copies)
    pre = join_halves(dot(x[...], enc2[...]), left) + bias_ref[...]
    pre_ref[...] = pre
    codes = split_halves(pre * jax.nn.sigmoid(pre), left).astype(BF)
    wait(dec_copies)
    for c in range(0, half, COLS):
        done[:, c : c + COLS] = dot(codes, dec2[:, c : c + COLS]).astype(BF)
    wait(start([(b, a) for a, b in moves(outs, done)], sems))


def encode_decode(x, enc, bias, dec):
    width, n = enc.shape
    half = width // 2
    parts = len(x)
    total = sum(a.shape[0] for a in x)
    return pl.pallas_call(
        functools.partial(code_kernel, parts),
        in_specs=[ANY] * (parts + 1) + [pl.BlockSpec(memory_space=pltpu.VMEM), ANY],
        out_specs=[ANY] * parts + [pl.BlockSpec(memory_space=pltpu.VMEM)],
        out_shape=[jax.ShapeDtypeStruct(a.shape, BF) for a in x]
        + [jax.ShapeDtypeStruct((total, n), F32)],
        scratch_shapes=[
            pltpu.VMEM((half, 2 * n), BF),
            pltpu.VMEM((2 * n, half), BF),
            pltpu.VMEM((total, half), BF),
            pltpu.VMEM((total, half), BF),
            pltpu.SemaphoreType.DMA((4,)),
            pltpu.SemaphoreType.DMA((SIDE,)),
            pltpu.SemaphoreType.DMA((SIDE,)),
        ],
        compiler_params=pltpu.CompilerParams(vmem_limit_bytes=16 * 1024 * 1024),
        name="encode_decode",
    )(*x, enc, bias, dec)


def slot_moves(refs, buffer):
    part = refs[0].shape[0]
    pairs = [(refs[k], buffer.at[k * part : (k + 1) * part]) for k in range(SIDE)]
    return pairs + [(refs[SIDE], buffer.at[SIDE * part :])]


def error_kernel(blocks, ids_ref, bias_ref, act_ref, *refs):
    ins, outs = refs[: SIDE + 1], refs[SIDE + 1 : 2 * SIDE + 2]
    act2, back, sel, err2, pieces, act_sems, in_sems, sems = refs[2 * SIDE + 2 :]
    n, width = act_ref.shape
    half = width // 2
    copies = start(slot_moves(ins, back), in_sems)
    copies += start(
        [(act_ref.at[:, s * half : (s + 1) * half], act2.at[s * n : (s + 1) * n]) for s in range(2)],
        act_sems,
    )
    sel[...] = one_hot_slots(ids_ref[...], blocks)
    wait(copies)
    step = COLS
    for c in range(0, half, step):
        sums = dot_t(sel[...], back[:, c : c + step])
        for s in range(2):
            rows = slice(s * n, (s + 1) * n)
            bias = bias_ref[:, s * half + c : s * half + c + step]
            wanted = act2[rows, c : c + step].astype(F32)
            err2[rows, c : c + step] = ((sums[rows] + bias - wanted) * (1.0 / 64.0)).astype(BF)
    send_slots(sel, err2, pieces, outs, sems)


def error_rows(ids, back, act, bias, blocks):
    n, width = act.shape
    half = width // 2
    total = 2 * blocks * PAIR
    in_vmem = pl.BlockSpec(memory_space=pltpu.VMEM)
    return pl.pallas_call(
        functools.partial(error_kernel, blocks),
        in_specs=[in_vmem, in_vmem] + [ANY] * (SIDE + 2),
        out_specs=[ANY] * (SIDE + 1),
        out_shape=slot_shapes(blocks, half),
        scratch_shapes=[
            pltpu.VMEM((2 * n, half), BF),
            pltpu.VMEM((total, half), BF),
            pltpu.VMEM((total, 2 * n), BF),
            pltpu.VMEM((2 * n, half), BF),
            pltpu.VMEM((total, half), BF),
            pltpu.SemaphoreType.DMA((2,)),
            pltpu.SemaphoreType.DMA((SIDE + 1,)),
            pltpu.SemaphoreType.DMA((SIDE + 1,)),
        ],
        compiler_params=PARAMS,
        name="error_rows",
    )(ids, bias, act, *back)


def hi_lo(x):
    hi = x.astype(BF).astype(F32)
    row = lax.broadcasted_iota(jnp.int32, (16, x.shape[1]), 0)
    return jnp.where(row == 0, hi, jnp.where(row == 1, x - hi, 0.0)).astype(BF)


def grad_kernel(pre_a, pre_b, dec_ref, *refs):
    x_refs, e_refs, outs = refs[: SIDE + 1], refs[SIDE + 1 : 2 * SIDE + 2], refs[2 * SIDE + 2 : 3 * SIDE + 2]
    dec2, x, e, pieces, w_sems, x_sems, e_sems, sems = refs[3 * SIDE + 2 :]
    rows, half = x.shape
    n = pre_a.shape[1]
    groups, _, quarter = pieces.shape
    e_copies = start(slot_moves(e_refs, e), e_sems)
    dec_copies = start(
        [(dec_ref.at[:, s * half : (s + 1) * half], dec2.at[s * n : (s + 1) * n]) for s in range(2)],
        w_sems,
    )
    x_copies = start(slot_moves(x_refs, x), x_sems)
    me = lax.axis_index("rows") // SIDE
    left = left_rows(rows)
    pre = jnp.concatenate([pre_b[...], pre_a[...]], axis=0)
    sig = jax.nn.sigmoid(pre)
    codes = split_halves(pre * sig, left).astype(BF)

    def fill(terms, slots, first):
        for g in range(groups // 2):
            both = dot_t(terms, slots[:, g * quarter : (g + 1) * quarter]).astype(BF)
            for s in range(2):
                pieces[g + s * (groups // 2), first : first + n, :] = both[s * n : (s + 1) * n]

    def give(first, last, turn):
        return start(
            [
                (pieces.at[lax.rem(me + k, SIDE), first:last], out.at[first:last])
                for k, out in enumerate(outs)
            ],
            sems,
            turn * SIDE,
        )

    wait(e_copies)
    fill(codes, e, 0)
    given = give(0, n, 0)
    wait(dec_copies)
    code_grad = join_halves(dot_nt(e[...], dec2[...]), left)
    grad = (code_grad * sig * (1.0 + pre * (1.0 - sig))).astype(BF).astype(F32)
    grads = split_halves(grad, left)
    bias = jnp.sum(grads[:, :n], axis=0, keepdims=True)
    wait(x_copies)
    fill(grads.astype(BF), x, n)
    for g in range(groups):
        shifted = pltpu.roll(bias, (n - g * (n // groups)) % n, 1)
        pieces[g, 2 * n :, :] = jnp.zeros((16, quarter), BF)
        pieces[g, 2 * n :, :n] = hi_lo(shifted)
    given += give(n, 2 * n + 16, 1)
    wait(given)


def hand_out(pieces, outs, me, sems):
    wait(start([(pieces.at[lax.rem(me + k, SIDE)], out) for k, out in enumerate(outs)], sems))


def gradients(x, err, pre_a, pre_b, dec):
    n, width = dec.shape
    piece = (2 * n + 16, width // SIDE)
    rows = 2 * pre_a.shape[0]
    in_vmem = pl.BlockSpec(memory_space=pltpu.VMEM)
    return pl.pallas_call(
        grad_kernel,
        in_specs=[in_vmem, in_vmem] + [ANY] * (2 * SIDE + 3),
        out_shape=[jax.ShapeDtypeStruct(piece, BF)] * SIDE,
        out_specs=[ANY] * SIDE,
        scratch_shapes=[
            pltpu.VMEM((2 * n, width // 2), BF),
            pltpu.VMEM((rows, width // 2), BF),
            pltpu.VMEM((rows, width // 2), BF),
            pltpu.VMEM((SIDE,) + piece, BF),
            pltpu.SemaphoreType.DMA((2,)),
            pltpu.SemaphoreType.DMA((SIDE + 1,)),
            pltpu.SemaphoreType.DMA((SIDE + 1,)),
            pltpu.SemaphoreType.DMA((2 * SIDE,)),
        ],
        compiler_params=PARAMS,
        name="gradients",
    )(pre_a, pre_b, dec, *x, *err)


def first_sum_kernel(*refs):
    ins, outs, (pieces, sems) = refs[:SIDE], refs[SIDE : 2 * SIDE], refs[2 * SIDE :]
    rows, quarter = ins[0].shape
    n = (rows - 16) // 2
    piece = pieces.shape[1] - 16
    total = ins[0][: 2 * n, :].astype(F32)
    bias = ins[0][2 * n :, :n].astype(F32)
    for part in ins[1:]:
        total = total + part[: 2 * n, :].astype(F32)
        bias = bias + part[2 * n :, :n].astype(F32)
    turned = total.T.astype(BF)
    bias = jnp.sum(bias, axis=0, keepdims=True)
    for c in range(SIDE):
        pieces[c, :piece, :] = turned[c * piece : (c + 1) * piece]
        shifted = pltpu.roll(bias, (n - c * (n // (SIDE * SIDE))) % n, 1)
        pieces[c, piece:, :n] = hi_lo(shifted)
        pieces[c, piece:, n:] = jnp.zeros((16, n), BF)
    hand_out(pieces, outs, lax.rem(lax.axis_index("rows"), SIDE), sems)


def first_sum(parts):
    rows, quarter = parts[0].shape
    piece = (quarter // SIDE + 16, rows - 16)
    return pl.pallas_call(
        first_sum_kernel,
        out_shape=[jax.ShapeDtypeStruct(piece, BF)] * SIDE,
        out_specs=[pl.BlockSpec(memory_space=pl.ANY)] * SIDE,
        scratch_shapes=[pltpu.VMEM((SIDE,) + piece, BF), pltpu.SemaphoreType.DMA((SIDE,))],
        compiler_params=PARAMS,
        name="sum_over_y",
    )(*parts)


def last_sum_kernel(*refs):
    ins, (enc_ref, dec_ref, bias_ref) = refs[:SIDE], refs[SIDE:]
    rows, cols = ins[0].shape
    piece, n = rows - 16, cols // 2
    total = ins[0][...].astype(F32)
    for part in ins[1:]:
        total = total + part[...].astype(F32)
    dec_ref[...] = total[:piece, :n]
    enc_ref[...] = total[:piece, n:]
    bias = jnp.sum(total[piece:, :n], axis=0, keepdims=True)
    bias_ref[...] = bias[:, : bias_ref.shape[1]]


def last_sum(parts, own):
    rows, cols = parts[0].shape
    piece, n = rows - 16, cols // 2
    return pl.pallas_call(
        last_sum_kernel,
        out_shape=[
            jax.ShapeDtypeStruct((piece, n), F32),
            jax.ShapeDtypeStruct((piece, n), F32),
            jax.ShapeDtypeStruct((1, own), F32),
        ],
        compiler_params=PARAMS,
        name="sum_over_z",
    )(*parts)


def share_pieces(pieces, along_y):
    got = [pieces[0]]
    for k in (2, 1, 3):
        pairs = []
        for i in range(SIDE * SIDE):
            y, z = divmod(i, SIDE)
            to = ((y + k) % SIDE, z) if along_y else (y, (z + k) % SIDE)
            pairs.append((i, to[0] * SIDE + to[1]))
        got.append(lax.ppermute(pieces[k], "rows", pairs))
    return got


def along_z(arrays, back=False):
    moved = {k: shift_z(arrays[k], STEPS[k], back) for k in (2, 1, 3)}
    return [arrays[0], moved[1], moved[2], moved[3]]


def shift_z(x, steps, back):
    pairs = []
    for i in range(512):
        rows, lat = divmod(i, 32)
        y, z_hi = divmod(rows, SIDE)
        x_place, rest = divmod(lat, 2 * SIDE)
        z_lo, core = divmod(rest, 2)
        step = -steps[core] if back else steps[core]
        z = (z_hi * SIDE + z_lo + step) % (SIDE * SIDE)
        to_rows = y * SIDE + z // SIDE
        pairs.append((i, to_rows * 32 + x_place * 2 * SIDE + z % SIDE * 2 + core))
    return lax.ppermute(x, ("rows", "lat"), pairs)


def over_x(x):
    groups = [
        [xp * 2 * SIDE + z * 2 + core for xp in range(SIDE) for core in range(2)]
        for z in range(SIDE)
    ]
    members = 2 * SIDE
    shape = x.shape
    out = lax.all_to_all(
        x.reshape(members, shape[0] // members, shape[1]),
        "lat",
        split_axis=0,
        concat_axis=0,
        axis_index_groups=groups,
        tiled=True,
    )
    return out.reshape(shape)


def to_owners(slots):
    moved = along_z(slots[:SIDE])
    crossed, merged = lax.optimization_barrier((over_x(slots[SIDE]), swap_pieces(moved, True)))
    stream_a = over_x(merged)
    stream_b = along_z(swap_pieces([crossed], False))
    return stream_a, stream_b


def to_homes(stream_a, stream_b):
    moved = along_z(stream_b, True)
    crossed, merged = lax.optimization_barrier((over_x(stream_a), swap_pieces(moved, True)))
    home_b = over_x(merged)
    home_a = along_z(swap_pieces([crossed], False), True)
    return [*home_a, home_b]


def local(activations, block_ids, enc_weight, enc_bias, dec_weight, dec_bias):
    blocks = lax.axis_size("lat")
    parts_rows = lax.axis_size("rows")
    n = enc_weight.shape[1]
    ids = block_ids.T
    bias = enc_bias[None, :]
    x_a, x_b = to_owners(pack(ids, activations, blocks))
    dec_a, pre_a = encode_decode([x_a], enc_weight, bias, dec_weight)
    x_b, dec_a = lax.optimization_barrier((x_b, dec_a))
    *dec_b, pre_b = encode_decode(x_b, enc_weight, bias, dec_weight)
    back = to_homes(dec_a, dec_b)
    e_a, e_b = to_owners(error_rows(ids, back, activations, dec_bias[None, :], blocks))
    terms = gradients([*x_b, x_a], [*e_b, e_a], pre_a, pre_b, dec_weight)
    terms = share_pieces(terms, True)
    terms = share_pieces(first_sum(terms), False)
    enc_grad, dec_turned, bias_grad = last_sum(terms, n // parts_rows)
    return enc_grad, dec_turned.T, bias_grad.reshape(-1)


def solution(mesh):
    in_specs = (
        P(("rows", "lat"), None),
        P(("rows", "lat"), None),
        P(None, "lat"),
        P("lat"),
        P("lat", None),
        P(),
    )
    out_specs = (P("rows", "lat"), P("lat", "rows"), P(("lat", "rows")))
    return jax.shard_map(local, mesh=mesh, in_specs=in_specs, out_specs=out_specs, check_vma=False)
```

```python
import functools

import jax
import jax.numpy as jnp
from jax import lax
from jax.experimental import pallas as pl
from jax.experimental.pallas import tpu as pltpu
from jax.sharding import PartitionSpec as P

SLOTS = 6
PAIR = 2 * SLOTS
SIDE = 4
STEPS = ((0, 0), (1, 1), (2, -2), (-1, -1))
BF = jnp.bfloat16
F32 = jnp.float32
VMEM = 56 * 1024 * 1024
COLS = 256
PARAMS = pltpu.CompilerParams(vmem_limit_bytes=VMEM)
ANY = pl.BlockSpec(memory_space=pl.ANY)


def by_twelve(row):
    return lax.shift_right_logical(row * 5462, 16)


def dot(a, b):
    return lax.dot_general(a, b, (((1,), (0,)), ((), ())), preferred_element_type=F32)


def dot_nt(a, b):
    return lax.dot_general(a, b, (((1,), (1,)), ((), ())), preferred_element_type=F32)


def left_rows(rows):
    row = lax.broadcasted_iota(jnp.int32, (rows, 1), 0)
    return row - by_twelve(row) * PAIR < SLOTS


def split_halves(x, left):
    zero = jnp.zeros_like(x)
    return jnp.concatenate([jnp.where(left, x, zero), jnp.where(left, zero, x)], axis=1)


def join_halves(y, left):
    rows, n = y.shape[0], y.shape[1] // 2
    yl, yr = y[:, :n], y[:, n:]
    after = pltpu.roll(yr, rows - SLOTS, 0)
    before = pltpu.roll(yl, SLOTS, 0)
    return jnp.where(left, yl + after, yr + before)


def one_hot_slots(ids, blocks):
    n = ids.shape[1]
    rows = 2 * blocks * PAIR
    number = lax.broadcasted_iota(jnp.int32, (blocks, n), 0)
    member = (number == ids[0:1, :]) | (number == ids[1:2, :])
    earlier = (
        lax.broadcasted_iota(jnp.int32, (n, n), 0) < lax.broadcasted_iota(jnp.int32, (n, n), 1)
    )
    position = dot(member.astype(F32).astype(BF), earlier.astype(F32).astype(BF))
    code = jnp.where(member, position, 200.0).astype(BF)
    zl = lax.rem(lax.axis_index("lat") // 2, SIDE)
    row = lax.broadcasted_iota(jnp.int32, (rows, 1), 0)
    piece = by_twelve(row)
    place = row - piece * PAIR
    first = piece < blocks
    in_a, in_b = piece, piece - blocks
    xc = jnp.where(first, in_a & 7, lax.shift_right_logical(in_b, 2))
    k = jnp.where(first, lax.shift_right_logical(in_a, 3), in_b & 3)
    block = lax.shift_right_logical(xc, 1) * (2 * SIDE) + ((zl + k) & 3) * 2 + (xc & 1)
    left = place < SLOTS
    slot = place - jnp.where(left, 0, SLOTS) + jnp.where(first, 0, SLOTS)
    expand = lax.broadcasted_iota(jnp.int32, (rows, blocks), 1) == block
    spread = dot(expand.astype(F32).astype(BF), code)
    hit = (spread == slot.astype(F32)).astype(F32)
    return split_halves(hit, left)


def start(pairs, sems, first=0):
    copies = [pltpu.make_async_copy(a, b, sems.at[first + i]) for i, (a, b) in enumerate(pairs)]
    for copy in copies:
        copy.start()
    return copies


def wait(copies):
    for copy in copies:
        copy.wait()


def send_slots(sel, rows2, slots, outs, sems):
    total, half = slots.shape
    rows = total // 2
    part = rows // SIDE
    copies = []
    for i in range(2):
        own = slice(i * rows, (i + 1) * rows)
        chosen = sel[own, :]
        for c in range(0, half, COLS):
            slots[own, c : c + COLS] = dot(chosen, rows2[:, c : c + COLS]).astype(BF)
        if i == 0:
            copies += start(
                [(slots.at[k * part : (k + 1) * part], outs[k]) for k in range(SIDE)], sems
            )
        else:
            copies += start([(slots.at[rows:], outs[SIDE])], sems, SIDE)
    wait(copies)


def slot_shapes(blocks, half):
    total = blocks * PAIR
    part = total // SIDE
    shapes = [jax.ShapeDtypeStruct((part, half), BF)] * SIDE
    return shapes + [jax.ShapeDtypeStruct((total, half), BF)]


def pack_kernel(blocks, ids_ref, act_ref, *refs):
    outs, (act2, sel, pieces, in_sems, sems) = refs[: SIDE + 1], refs[SIDE + 1 :]
    n, width = act_ref.shape
    half = width // 2
    copies = start(
        [(act_ref.at[:, s * half : (s + 1) * half], act2.at[s * n : (s + 1) * n]) for s in range(2)],
        in_sems,
    )
    sel[...] = one_hot_slots(ids_ref[...], blocks).astype(BF)
    wait(copies)
    send_slots(sel, act2, pieces, outs, sems)


def pack(ids, act, blocks):
    n, width = act.shape
    half = width // 2
    part = blocks * PAIR // SIDE
    return pl.pallas_call(
        functools.partial(pack_kernel, blocks),
        in_specs=[pl.BlockSpec(memory_space=pltpu.VMEM), ANY],
        out_specs=[ANY] * (SIDE + 1),
        out_shape=slot_shapes(blocks, half),
        scratch_shapes=[
            pltpu.VMEM((2 * n, half), BF),
            pltpu.VMEM((2 * SIDE * part, 2 * n), BF),
            pltpu.VMEM((2 * SIDE * part, half), BF),
            pltpu.SemaphoreType.DMA((2,)),
            pltpu.SemaphoreType.DMA((SIDE + 1,)),
        ],
        compiler_params=PARAMS,
        name="pack_rows",
    )(ids, act)


def swap_kernel(merge, *refs):
    if merge:
        ins, out_ref, (pieces, done, in_sems, sems) = refs[:SIDE], refs[SIDE], refs[SIDE + 1 :]
    else:
        in_ref, outs, (pieces, done, in_sems, sems) = refs[0], refs[1 : SIDE + 1], refs[SIDE + 1 :]
    rows = pieces.shape[1]
    part = rows // SIDE
    halves = range(2)
    if merge:
        moves = [
            [
                (ins[k].at[h * part : (h + 1) * part], pieces.at[h, k * part : (k + 1) * part])
                for k in range(SIDE)
            ]
            for h in halves
        ]
    else:
        moves = [[(in_ref.at[h * rows : (h + 1) * rows], pieces.at[h])] for h in halves]
    copies = [start(moves[h], in_sems, h * SIDE) for h in halves]
    row = lax.broadcasted_iota(jnp.int32, (rows, 1), 0)
    piece = by_twelve(row)
    source = (piece & 3) * part + lax.shift_right_logical(piece, 2) * PAIR + row - piece * PAIR
    turn = (lax.broadcasted_iota(jnp.int32, (rows, rows), 1) == source).astype(F32).astype(BF)
    sent = []
    for h in halves:
        wait(copies[h])
        done[h] = dot(turn, pieces[h]).astype(BF)
        if merge:
            sent += start([(done.at[h], out_ref.at[h * rows : (h + 1) * rows])], sems, h * SIDE)
        else:
            sent += start(
                [
                    (done.at[h, k * part : (k + 1) * part], outs[k].at[h * part : (h + 1) * part])
                    for k in range(SIDE)
                ],
                sems,
                h * SIDE,
            )
    wait(sent)


def swap_pieces(arrays, merge):
    total = arrays[0].shape[0] * (SIDE if merge else 1)
    half = arrays[0].shape[1]
    shape = jax.ShapeDtypeStruct((total, half), BF)
    shapes = [jax.ShapeDtypeStruct((total // SIDE, half), BF)] * SIDE
    return pl.pallas_call(
        functools.partial(swap_kernel, merge),
        in_specs=[ANY] * len(arrays),
        out_specs=ANY if merge else [ANY] * SIDE,
        out_shape=shape if merge else shapes,
        scratch_shapes=[
            pltpu.VMEM((2, total // 2, half), BF),
            pltpu.VMEM((2, total // 2, half), BF),
            pltpu.SemaphoreType.DMA((2 * SIDE,)),
            pltpu.SemaphoreType.DMA((2 * SIDE,)),
        ],
        compiler_params=PARAMS,
        name="merge_pieces" if merge else "split_pieces",
    )(*arrays)


def code_kernel(parts, *refs):
    ins, (enc_ref, bias_ref, dec_ref) = refs[:parts], refs[parts : parts + 3]
    outs, pre_ref = refs[parts + 3 : 2 * parts + 3], refs[2 * parts + 3]
    enc2, dec2, x, done, w_sems, in_sems, sems = refs[2 * parts + 4 :]
    half, n = enc2.shape[0], enc2.shape[1] // 2
    total = x.shape[0]
    rows = total // parts

    def moves(refs, buffer):
        return [(refs[i], buffer.at[i * rows : (i + 1) * rows]) for i in range(parts)]

    enc_copies = start(
        [(enc_ref.at[s * half : (s + 1) * half], enc2.at[:, s * n : (s + 1) * n]) for s in range(2)],
        w_sems,
    )
    in_copies = start(moves(ins, x), in_sems)
    dec_copies = start(
        [(dec_ref.at[:, s * half : (s + 1) * half], dec2.at[s * n : (s + 1) * n]) for s in range(2)],
        w_sems,
        2,
    )
    left = left_rows(total)
    wait(enc_copies)
    wait(in_copies)
    pre = join_halves(dot(x[...], enc2[...]), left) + bias_ref[...]
    pre_ref[...] = pre
    codes = split_halves(pre * jax.nn.sigmoid(pre), left).astype(BF)
    wait(dec_copies)
    for c in range(0, half, COLS):
        done[:, c : c + COLS] = dot(codes, dec2[:, c : c + COLS]).astype(BF)
    wait(start([(b, a) for a, b in moves(outs, done)], sems))


def encode_decode(x, enc, bias, dec):
    width, n = enc.shape
    half = width // 2
    parts = len(x)
    total = sum(a.shape[0] for a in x)
    return pl.pallas_call(
        functools.partial(code_kernel, parts),
        in_specs=[ANY] * (parts + 1) + [pl.BlockSpec(memory_space=pltpu.VMEM), ANY],
        out_specs=[ANY] * parts + [pl.BlockSpec(memory_space=pltpu.VMEM)],
        out_shape=[jax.ShapeDtypeStruct(a.shape, BF) for a in x]
        + [jax.ShapeDtypeStruct((total, n), F32)],
        scratch_shapes=[
            pltpu.VMEM((half, 2 * n), BF),
            pltpu.VMEM((2 * n, half), BF),
            pltpu.VMEM((total, half), BF),
            pltpu.VMEM((total, half), BF),
            pltpu.SemaphoreType.DMA((4,)),
            pltpu.SemaphoreType.DMA((SIDE,)),
            pltpu.SemaphoreType.DMA((SIDE,)),
        ],
        compiler_params=pltpu.CompilerParams(vmem_limit_bytes=16 * 1024 * 1024),
        name="encode_decode",
    )(*x, enc, bias, dec)


def slot_moves(refs, buffer):
    part = refs[0].shape[0]
    pairs = [(refs[k], buffer.at[k * part : (k + 1) * part]) for k in range(SIDE)]
    return pairs + [(refs[SIDE], buffer.at[SIDE * part :])]


def error_kernel(blocks, ids_ref, bias_ref, act_ref, *refs):
    ins, outs = refs[: SIDE + 1], refs[SIDE + 1 : 2 * SIDE + 2]
    act2, back, sel, err2, pieces, act_sems, in_sems, sems = refs[2 * SIDE + 2 :]
    n, width = act_ref.shape
    half = width // 2
    copies = start(slot_moves(ins, back), in_sems)
    copies += start(
        [(act_ref.at[:, s * half : (s + 1) * half], act2.at[s * n : (s + 1) * n]) for s in range(2)],
        act_sems,
    )
    hits = one_hot_slots(ids_ref[...], blocks)
    sel[...] = hits.astype(BF)
    turned = hits.T.astype(BF)
    wait(copies)
    step = COLS
    for c in range(0, half, step):
        sums = dot(turned, back[:, c : c + step])
        for s in range(2):
            rows = slice(s * n, (s + 1) * n)
            bias = bias_ref[:, s * half + c : s * half + c + step]
            wanted = act2[rows, c : c + step].astype(F32)
            err2[rows, c : c + step] = ((sums[rows] + bias - wanted) * (1.0 / 64.0)).astype(BF)
    send_slots(sel, err2, pieces, outs, sems)


def error_rows(ids, back, act, bias, blocks):
    n, width = act.shape
    half = width // 2
    total = 2 * blocks * PAIR
    in_vmem = pl.BlockSpec(memory_space=pltpu.VMEM)
    return pl.pallas_call(
        functools.partial(error_kernel, blocks),
        in_specs=[in_vmem, in_vmem] + [ANY] * (SIDE + 2),
        out_specs=[ANY] * (SIDE + 1),
        out_shape=slot_shapes(blocks, half),
        scratch_shapes=[
            pltpu.VMEM((2 * n, half), BF),
            pltpu.VMEM((total, half), BF),
            pltpu.VMEM((total, 2 * n), BF),
            pltpu.VMEM((2 * n, half), BF),
            pltpu.VMEM((total, half), BF),
            pltpu.SemaphoreType.DMA((2,)),
            pltpu.SemaphoreType.DMA((SIDE + 1,)),
            pltpu.SemaphoreType.DMA((SIDE + 1,)),
        ],
        compiler_params=PARAMS,
        name="error_rows",
    )(ids, bias, act, *back)


def hi_lo(x):
    hi = x.astype(BF).astype(F32)
    row = lax.broadcasted_iota(jnp.int32, (16, x.shape[1]), 0)
    return jnp.where(row == 0, hi, jnp.where(row == 1, x - hi, 0.0)).astype(BF)


def grad_kernel(pre_a, pre_b, dec_ref, *refs):
    x_refs, e_refs, outs = refs[: SIDE + 1], refs[SIDE + 1 : 2 * SIDE + 2], refs[2 * SIDE + 2 : 3 * SIDE + 2]
    dec2, x, e, pieces, w_sems, x_sems, e_sems, sems = refs[3 * SIDE + 2 :]
    rows, half = x.shape
    n = pre_a.shape[1]
    groups, _, quarter = pieces.shape
    e_copies = start(slot_moves(e_refs, e), e_sems)
    dec_copies = start(
        [(dec_ref.at[:, s * half : (s + 1) * half], dec2.at[s * n : (s + 1) * n]) for s in range(2)],
        w_sems,
    )
    x_copies = start(slot_moves(x_refs, x), x_sems)
    me = lax.axis_index("rows") // SIDE
    left = left_rows(rows)
    pre = jnp.concatenate([pre_b[...], pre_a[...]], axis=0)
    sig = jax.nn.sigmoid(pre)
    codes = split_halves((pre * sig).astype(BF).astype(F32), left)

    def fill(terms, slots, first):
        turned = terms.T.astype(BF)
        for g in range(groups // 2):
            both = dot(turned, slots[:, g * quarter : (g + 1) * quarter]).astype(BF)
            for s in range(2):
                pieces[g + s * (groups // 2), first : first + n, :] = both[s * n : (s + 1) * n]

    def give(first, last, turn):
        return start(
            [
                (pieces.at[lax.rem(me + k, SIDE), first:last], out.at[first:last])
                for k, out in enumerate(outs)
            ],
            sems,
            turn * SIDE,
        )

    wait(e_copies)
    fill(codes, e, 0)
    given = give(0, n, 0)
    wait(dec_copies)
    code_grad = join_halves(dot_nt(e[...], dec2[...]), left)
    grad = (code_grad * sig * (1.0 + pre * (1.0 - sig))).astype(BF).astype(F32)
    grads = split_halves(grad, left)
    bias = jnp.sum(grads[:, :n], axis=0, keepdims=True)
    wait(x_copies)
    fill(grads, x, n)
    for g in range(groups):
        shifted = pltpu.roll(bias, (n - g * (n // groups)) % n, 1)
        pieces[g, 2 * n :, :] = jnp.zeros((16, quarter), BF)
        pieces[g, 2 * n :, :n] = hi_lo(shifted)
    given += give(n, 2 * n + 16, 1)
    wait(given)


def hand_out(pieces, outs, me, sems):
    wait(start([(pieces.at[lax.rem(me + k, SIDE)], out) for k, out in enumerate(outs)], sems))


def gradients(x, err, pre_a, pre_b, dec):
    n, width = dec.shape
    piece = (2 * n + 16, width // SIDE)
    rows = 2 * pre_a.shape[0]
    in_vmem = pl.BlockSpec(memory_space=pltpu.VMEM)
    return pl.pallas_call(
        grad_kernel,
        in_specs=[in_vmem, in_vmem] + [ANY] * (2 * SIDE + 3),
        out_shape=[jax.ShapeDtypeStruct(piece, BF)] * SIDE,
        out_specs=[ANY] * SIDE,
        scratch_shapes=[
            pltpu.VMEM((2 * n, width // 2), BF),
            pltpu.VMEM((rows, width // 2), BF),
            pltpu.VMEM((rows, width // 2), BF),
            pltpu.VMEM((SIDE,) + piece, BF),
            pltpu.SemaphoreType.DMA((2,)),
            pltpu.SemaphoreType.DMA((SIDE + 1,)),
            pltpu.SemaphoreType.DMA((SIDE + 1,)),
            pltpu.SemaphoreType.DMA((2 * SIDE,)),
        ],
        compiler_params=PARAMS,
        name="gradients",
    )(pre_a, pre_b, dec, *x, *err)


def first_sum_kernel(*refs):
    ins, outs, (pieces, sems) = refs[:SIDE], refs[SIDE : 2 * SIDE], refs[2 * SIDE :]
    rows, quarter = ins[0].shape
    n = (rows - 16) // 2
    piece = pieces.shape[1] - 16
    total = ins[0][: 2 * n, :].astype(F32)
    bias = ins[0][2 * n :, :n].astype(F32)
    for part in ins[1:]:
        total = total + part[: 2 * n, :].astype(F32)
        bias = bias + part[2 * n :, :n].astype(F32)
    turned = total.T.astype(BF)
    bias = jnp.sum(bias, axis=0, keepdims=True)
    for c in range(SIDE):
        pieces[c, :piece, :] = turned[c * piece : (c + 1) * piece]
        shifted = pltpu.roll(bias, (n - c * (n // (SIDE * SIDE))) % n, 1)
        pieces[c, piece:, :n] = hi_lo(shifted)
        pieces[c, piece:, n:] = jnp.zeros((16, n), BF)
    hand_out(pieces, outs, lax.rem(lax.axis_index("rows"), SIDE), sems)


def first_sum(parts):
    rows, quarter = parts[0].shape
    piece = (quarter // SIDE + 16, rows - 16)
    return pl.pallas_call(
        first_sum_kernel,
        out_shape=[jax.ShapeDtypeStruct(piece, BF)] * SIDE,
        out_specs=[pl.BlockSpec(memory_space=pl.ANY)] * SIDE,
        scratch_shapes=[pltpu.VMEM((SIDE,) + piece, BF), pltpu.SemaphoreType.DMA((SIDE,))],
        compiler_params=PARAMS,
        name="sum_over_y",
    )(*parts)


def last_sum_kernel(*refs):
    ins, (enc_ref, dec_ref, bias_ref) = refs[:SIDE], refs[SIDE:]
    rows, cols = ins[0].shape
    piece, n = rows - 16, cols // 2
    total = ins[0][...].astype(F32)
    for part in ins[1:]:
        total = total + part[...].astype(F32)
    dec_ref[...] = total[:piece, :n]
    enc_ref[...] = total[:piece, n:]
    bias = jnp.sum(total[piece:, :n], axis=0, keepdims=True)
    bias_ref[...] = bias[:, : bias_ref.shape[1]]


def last_sum(parts, own):
    rows, cols = parts[0].shape
    piece, n = rows - 16, cols // 2
    return pl.pallas_call(
        last_sum_kernel,
        out_shape=[
            jax.ShapeDtypeStruct((piece, n), F32),
            jax.ShapeDtypeStruct((piece, n), F32),
            jax.ShapeDtypeStruct((1, own), F32),
        ],
        compiler_params=PARAMS,
        name="sum_over_z",
    )(*parts)


def share_pieces(pieces, along_y):
    got = [pieces[0]]
    for k in (2, 1, 3):
        pairs = []
        for i in range(SIDE * SIDE):
            y, z = divmod(i, SIDE)
            to = ((y + k) % SIDE, z) if along_y else (y, (z + k) % SIDE)
            pairs.append((i, to[0] * SIDE + to[1]))
        got.append(lax.ppermute(pieces[k], "rows", pairs))
    return got


def along_z(arrays, back=False):
    moved = {k: shift_z(arrays[k], STEPS[k], back) for k in (2, 1, 3)}
    return [arrays[0], moved[1], moved[2], moved[3]]


def shift_z(x, steps, back):
    pairs = []
    for i in range(512):
        rows, lat = divmod(i, 32)
        y, z_hi = divmod(rows, SIDE)
        x_place, rest = divmod(lat, 2 * SIDE)
        z_lo, core = divmod(rest, 2)
        step = -steps[core] if back else steps[core]
        z = (z_hi * SIDE + z_lo + step) % (SIDE * SIDE)
        to_rows = y * SIDE + z // SIDE
        pairs.append((i, to_rows * 32 + x_place * 2 * SIDE + z % SIDE * 2 + core))
    return lax.ppermute(x, ("rows", "lat"), pairs)


def over_x(x):
    groups = [
        [xp * 2 * SIDE + z * 2 + core for xp in range(SIDE) for core in range(2)]
        for z in range(SIDE)
    ]
    members = 2 * SIDE
    shape = x.shape
    out = lax.all_to_all(
        x.reshape(members, shape[0] // members, shape[1]),
        "lat",
        split_axis=0,
        concat_axis=0,
        axis_index_groups=groups,
        tiled=True,
    )
    return out.reshape(shape)


def to_owners(slots):
    moved = along_z(slots[:SIDE])
    pieces = swap_pieces([over_x(slots[SIDE])], False)
    pieces, moved = lax.optimization_barrier((pieces, moved))
    stream_a = over_x(swap_pieces(moved, True))
    stream_b = along_z(pieces)
    return stream_a, stream_b


def to_homes(stream_a, stream_b):
    moved = along_z(stream_b, True)
    pieces = swap_pieces([over_x(stream_a)], False)
    pieces, moved = lax.optimization_barrier((pieces, moved))
    home_b = over_x(swap_pieces(moved, True))
    home_a = along_z(pieces, True)
    return [*home_a, home_b]


def local(activations, block_ids, enc_weight, enc_bias, dec_weight, dec_bias):
    blocks = lax.axis_size("lat")
    parts_rows = lax.axis_size("rows")
    n = enc_weight.shape[1]
    ids = block_ids.T
    bias = enc_bias[None, :]
    x_a, x_b = to_owners(pack(ids, activations, blocks))
    dec_a, pre_a = encode_decode([x_a], enc_weight, bias, dec_weight)
    x_b, dec_a = lax.optimization_barrier((x_b, dec_a))
    *dec_b, pre_b = encode_decode(x_b, enc_weight, bias, dec_weight)
    back = to_homes(dec_a, dec_b)
    e_a, e_b = to_owners(error_rows(ids, back, activations, dec_bias[None, :], blocks))
    terms = gradients([*x_b, x_a], [*e_b, e_a], pre_a, pre_b, dec_weight)
    terms = share_pieces(terms, True)
    terms = share_pieces(first_sum(terms), False)
    enc_grad, dec_turned, bias_grad = last_sum(terms, n // parts_rows)
    return enc_grad, dec_turned.T, bias_grad.reshape(-1)


def solution(mesh):
    in_specs = (
        P(("rows", "lat"), None),
        P(("rows", "lat"), None),
        P(None, "lat"),
        P("lat"),
        P("lat", None),
        P(),
    )
    out_specs = (P("rows", "lat"), P("lat", "rows"), P(("lat", "rows")))
    return jax.shard_map(local, mesh=mesh, in_specs=in_specs, out_specs=out_specs, check_vma=False)
```

```python
import functools

import jax
import jax.numpy as jnp
from jax import lax
from jax.experimental import pallas as pl
from jax.experimental.pallas import tpu as pltpu
from jax.sharding import PartitionSpec as P

SLOTS = 6
PAIR = 2 * SLOTS
SIDE = 4
STEPS = ((0, 0), (1, 1), (2, -2), (-1, -1))
BF = jnp.bfloat16
F32 = jnp.float32
VMEM = 56 * 1024 * 1024
COLS = 256
PARAMS = pltpu.CompilerParams(vmem_limit_bytes=VMEM)
ANY = pl.BlockSpec(memory_space=pl.ANY)


def by_twelve(row):
    return lax.shift_right_logical(row * 5462, 16)


def dot(a, b):
    return lax.dot_general(a, b, (((1,), (0,)), ((), ())), preferred_element_type=F32)


def dot_nt(a, b):
    return lax.dot_general(a, b, (((1,), (1,)), ((), ())), preferred_element_type=F32)


def left_rows(rows):
    row = lax.broadcasted_iota(jnp.int32, (rows, 1), 0)
    return row - by_twelve(row) * PAIR < SLOTS


def split_halves(x, left):
    zero = jnp.zeros_like(x)
    return jnp.concatenate([jnp.where(left, x, zero), jnp.where(left, zero, x)], axis=1)


def join_halves(y, left):
    rows, n = y.shape[0], y.shape[1] // 2
    yl, yr = y[:, :n], y[:, n:]
    after = pltpu.roll(yr, rows - SLOTS, 0)
    before = pltpu.roll(yl, SLOTS, 0)
    return jnp.where(left, yl + after, yr + before)


def one_hot_slots(ids, blocks):
    n = ids.shape[1]
    rows = 2 * blocks * PAIR
    number = lax.broadcasted_iota(jnp.int32, (blocks, n), 0)
    member = (number == ids[0:1, :]) | (number == ids[1:2, :])
    earlier = (
        lax.broadcasted_iota(jnp.int32, (n, n), 0) < lax.broadcasted_iota(jnp.int32, (n, n), 1)
    )
    position = dot(member.astype(F32).astype(BF), earlier.astype(F32).astype(BF))
    code = jnp.where(member, position, 200.0).astype(BF)
    zl = lax.rem(lax.axis_index("lat") // 2, SIDE)
    row = lax.broadcasted_iota(jnp.int32, (rows, 1), 0)
    piece = by_twelve(row)
    place = row - piece * PAIR
    first = piece < blocks
    in_a, in_b = piece, piece - blocks
    xc = jnp.where(first, in_a & 7, lax.shift_right_logical(in_b, 2))
    k = jnp.where(first, lax.shift_right_logical(in_a, 3), in_b & 3)
    block = lax.shift_right_logical(xc, 1) * (2 * SIDE) + ((zl + k) & 3) * 2 + (xc & 1)
    left = place < SLOTS
    slot = place - jnp.where(left, 0, SLOTS) + jnp.where(first, 0, SLOTS)
    expand = lax.broadcasted_iota(jnp.int32, (rows, blocks), 1) == block
    spread = dot(expand.astype(F32).astype(BF), code)
    hit = (spread == slot.astype(F32)).astype(F32)
    return split_halves(hit, left)


def start(pairs, sems, first=0):
    copies = [pltpu.make_async_copy(a, b, sems.at[first + i]) for i, (a, b) in enumerate(pairs)]
    for copy in copies:
        copy.start()
    return copies


def wait(copies):
    for copy in copies:
        copy.wait()


def send_slots(sel, rows2, slots, outs, sems):
    total, half = slots.shape
    rows = total // 2
    part = rows // SIDE
    copies = []
    for i in range(2):
        own = slice(i * rows, (i + 1) * rows)
        chosen = sel[own, :]
        for c in range(0, half, COLS):
            slots[own, c : c + COLS] = dot(chosen, rows2[:, c : c + COLS]).astype(BF)
        if i == 0:
            copies += start(
                [(slots.at[k * part : (k + 1) * part], outs[k]) for k in range(SIDE)], sems
            )
        else:
            copies += start([(slots.at[rows:], outs[SIDE])], sems, SIDE)
    wait(copies)


def slot_shapes(blocks, half):
    total = blocks * PAIR
    part = total // SIDE
    shapes = [jax.ShapeDtypeStruct((part, half), BF)] * SIDE
    return shapes + [jax.ShapeDtypeStruct((total, half), BF)]


def pack_kernel(blocks, ids_ref, act_ref, *refs):
    outs, (act2, sel, pieces, in_sems, sems) = refs[: SIDE + 1], refs[SIDE + 1 :]
    n, width = act_ref.shape
    half = width // 2
    copies = start(
        [(act_ref.at[:, s * half : (s + 1) * half], act2.at[s * n : (s + 1) * n]) for s in range(2)],
        in_sems,
    )
    sel[...] = one_hot_slots(ids_ref[...], blocks).astype(BF)
    wait(copies)
    send_slots(sel, act2, pieces, outs, sems)


def pack(ids, act, blocks):
    n, width = act.shape
    half = width // 2
    part = blocks * PAIR // SIDE
    return pl.pallas_call(
        functools.partial(pack_kernel, blocks),
        in_specs=[pl.BlockSpec(memory_space=pltpu.VMEM), ANY],
        out_specs=[ANY] * (SIDE + 1),
        out_shape=slot_shapes(blocks, half),
        scratch_shapes=[
            pltpu.VMEM((2 * n, half), BF),
            pltpu.VMEM((2 * SIDE * part, 2 * n), BF),
            pltpu.VMEM((2 * SIDE * part, half), BF),
            pltpu.SemaphoreType.DMA((2,)),
            pltpu.SemaphoreType.DMA((SIDE + 1,)),
        ],
        compiler_params=PARAMS,
        name="pack_rows",
    )(ids, act)


def turn_kernel(*refs):
    moved, crossed, merged, split = refs[:SIDE], refs[SIDE], refs[SIDE + 1], refs[SIDE + 2 : -4]
    pieces, done, in_sems, sems = refs[-4:]
    rows = pieces.shape[1]
    part = rows // SIDE

    def by_step(arrays, buffer, h):
        return [
            (arrays[k].at[h * part : (h + 1) * part], buffer.at[h, k * part : (k + 1) * part])
            for k in range(SIDE)
        ]

    copies = [start(by_step(moved, pieces, h), in_sems, h * SIDE) for h in range(2)]
    copies += [
        start([(crossed.at[h * rows : (h + 1) * rows], pieces.at[2 + h])], in_sems, 2 * SIDE + h)
        for h in range(2)
    ]
    row = lax.broadcasted_iota(jnp.int32, (rows, 1), 0)
    piece = by_twelve(row)
    source = (piece & 3) * part + lax.shift_right_logical(piece, 2) * PAIR + row - piece * PAIR
    turn = (lax.broadcasted_iota(jnp.int32, (rows, rows), 1) == source).astype(F32).astype(BF)
    sent = []
    for i in range(4):
        wait(copies[i])
        done[i] = dot(turn, pieces[i]).astype(BF)
        if i < 2:
            pairs = [(done.at[i], merged.at[i * rows : (i + 1) * rows])]
        else:
            pairs = [(b, a) for a, b in by_step(split, done.at[2:], i - 2)]
        sent += start(pairs, sems, i * SIDE)
    wait(sent)


def turn_pieces(moved, crossed):
    total, half = crossed.shape
    shape = jax.ShapeDtypeStruct((total, half), BF)
    shapes = [jax.ShapeDtypeStruct((total // SIDE, half), BF)] * SIDE
    merged, *split = pl.pallas_call(
        turn_kernel,
        in_specs=[ANY] * (SIDE + 1),
        out_specs=[ANY] * (SIDE + 1),
        out_shape=[shape] + shapes,
        scratch_shapes=[
            pltpu.VMEM((4, total // 2, half), BF),
            pltpu.VMEM((4, total // 2, half), BF),
            pltpu.SemaphoreType.DMA((2 * SIDE + 2,)),
            pltpu.SemaphoreType.DMA((4 * SIDE,)),
        ],
        compiler_params=PARAMS,
        name="turn_pieces",
    )(*moved, crossed)
    return merged, split


def code_kernel(parts, *refs):
    ins, (enc_ref, bias_ref, dec_ref) = refs[:parts], refs[parts : parts + 3]
    outs, pre_ref = refs[parts + 3 : 2 * parts + 3], refs[2 * parts + 3]
    enc2, dec2, x, done, w_sems, in_sems, sems = refs[2 * parts + 4 :]
    half, n = enc2.shape[0], enc2.shape[1] // 2
    total = x.shape[0]
    rows = total // parts

    def moves(refs, buffer):
        return [(refs[i], buffer.at[i * rows : (i + 1) * rows]) for i in range(parts)]

    enc_copies = start(
        [(enc_ref.at[s * half : (s + 1) * half], enc2.at[:, s * n : (s + 1) * n]) for s in range(2)],
        w_sems,
    )
    in_copies = start(moves(ins, x), in_sems)
    dec_copies = start(
        [(dec_ref.at[:, s * half : (s + 1) * half], dec2.at[s * n : (s + 1) * n]) for s in range(2)],
        w_sems,
        2,
    )
    left = left_rows(total)
    wait(enc_copies)
    wait(in_copies)
    pre = join_halves(dot(x[...], enc2[...]), left) + bias_ref[...]
    pre_ref[...] = pre
    codes = split_halves(pre * jax.nn.sigmoid(pre), left).astype(BF)
    wait(dec_copies)
    for c in range(0, half, COLS):
        done[:, c : c + COLS] = dot(codes, dec2[:, c : c + COLS]).astype(BF)
    wait(start([(b, a) for a, b in moves(outs, done)], sems))


def encode_decode(x, enc, bias, dec):
    width, n = enc.shape
    half = width // 2
    parts = len(x)
    total = sum(a.shape[0] for a in x)
    return pl.pallas_call(
        functools.partial(code_kernel, parts),
        in_specs=[ANY] * (parts + 1) + [pl.BlockSpec(memory_space=pltpu.VMEM), ANY],
        out_specs=[ANY] * parts + [pl.BlockSpec(memory_space=pltpu.VMEM)],
        out_shape=[jax.ShapeDtypeStruct(a.shape, BF) for a in x]
        + [jax.ShapeDtypeStruct((total, n), F32)],
        scratch_shapes=[
            pltpu.VMEM((half, 2 * n), BF),
            pltpu.VMEM((2 * n, half), BF),
            pltpu.VMEM((total, half), BF),
            pltpu.VMEM((total, half), BF),
            pltpu.SemaphoreType.DMA((4,)),
            pltpu.SemaphoreType.DMA((SIDE,)),
            pltpu.SemaphoreType.DMA((SIDE,)),
        ],
        compiler_params=pltpu.CompilerParams(vmem_limit_bytes=16 * 1024 * 1024),
        name="encode_decode",
    )(*x, enc, bias, dec)


def slot_moves(refs, buffer):
    part = refs[0].shape[0]
    pairs = [(refs[k], buffer.at[k * part : (k + 1) * part]) for k in range(SIDE)]
    return pairs + [(refs[SIDE], buffer.at[SIDE * part :])]


def error_kernel(blocks, ids_ref, bias_ref, act_ref, *refs):
    ins, outs = refs[: SIDE + 1], refs[SIDE + 1 : 2 * SIDE + 2]
    act2, back, sel, err2, pieces, act_sems, in_sems, sems = refs[2 * SIDE + 2 :]
    n, width = act_ref.shape
    half = width // 2
    copies = start(slot_moves(ins, back), in_sems)
    copies += start(
        [(act_ref.at[:, s * half : (s + 1) * half], act2.at[s * n : (s + 1) * n]) for s in range(2)],
        act_sems,
    )
    hits = one_hot_slots(ids_ref[...], blocks)
    sel[...] = hits.astype(BF)
    turned = hits.T.astype(BF)
    wait(copies)
    step = COLS
    for c in range(0, half, step):
        sums = dot(turned, back[:, c : c + step])
        for s in range(2):
            rows = slice(s * n, (s + 1) * n)
            bias = bias_ref[:, s * half + c : s * half + c + step]
            wanted = act2[rows, c : c + step].astype(F32)
            err2[rows, c : c + step] = ((sums[rows] + bias - wanted) * (1.0 / 64.0)).astype(BF)
    send_slots(sel, err2, pieces, outs, sems)


def error_rows(ids, back, act, bias, blocks):
    n, width = act.shape
    half = width // 2
    total = 2 * blocks * PAIR
    in_vmem = pl.BlockSpec(memory_space=pltpu.VMEM)
    return pl.pallas_call(
        functools.partial(error_kernel, blocks),
        in_specs=[in_vmem, in_vmem] + [ANY] * (SIDE + 2),
        out_specs=[ANY] * (SIDE + 1),
        out_shape=slot_shapes(blocks, half),
        scratch_shapes=[
            pltpu.VMEM((2 * n, half), BF),
            pltpu.VMEM((total, half), BF),
            pltpu.VMEM((total, 2 * n), BF),
            pltpu.VMEM((2 * n, half), BF),
            pltpu.VMEM((total, half), BF),
            pltpu.SemaphoreType.DMA((2,)),
            pltpu.SemaphoreType.DMA((SIDE + 1,)),
            pltpu.SemaphoreType.DMA((SIDE + 1,)),
        ],
        compiler_params=PARAMS,
        name="error_rows",
    )(ids, bias, act, *back)


def hi_lo(x):
    hi = x.astype(BF).astype(F32)
    row = lax.broadcasted_iota(jnp.int32, (16, x.shape[1]), 0)
    return jnp.where(row == 0, hi, jnp.where(row == 1, x - hi, 0.0)).astype(BF)


def grad_kernel(pre_a, pre_b, dec_ref, *refs):
    x_refs, e_refs, outs = refs[: SIDE + 1], refs[SIDE + 1 : 2 * SIDE + 2], refs[2 * SIDE + 2 : 3 * SIDE + 2]
    dec2, x, e, pieces, w_sems, x_sems, e_sems, sems = refs[3 * SIDE + 2 :]
    rows, half = x.shape
    n = pre_a.shape[1]
    groups, _, quarter = pieces.shape
    e_copies = start(slot_moves(e_refs, e), e_sems)
    dec_copies = start(
        [(dec_ref.at[:, s * half : (s + 1) * half], dec2.at[s * n : (s + 1) * n]) for s in range(2)],
        w_sems,
    )
    x_copies = start(slot_moves(x_refs, x), x_sems)
    me = lax.axis_index("rows") // SIDE
    left = left_rows(rows)
    pre = jnp.concatenate([pre_b[...], pre_a[...]], axis=0)
    sig = jax.nn.sigmoid(pre)
    codes = split_halves((pre * sig).astype(BF).astype(F32), left)

    def fill(terms, slots, first):
        turned = terms.T.astype(BF)
        for g in range(groups // 2):
            both = dot(turned, slots[:, g * quarter : (g + 1) * quarter]).astype(BF)
            for s in range(2):
                pieces[g + s * (groups // 2), first : first + n, :] = both[s * n : (s + 1) * n]

    def give(first, last, turn):
        return start(
            [
                (pieces.at[lax.rem(me + k, SIDE), first:last], out.at[first:last])
                for k, out in enumerate(outs)
            ],
            sems,
            turn * SIDE,
        )

    wait(e_copies)
    fill(codes, e, 0)
    given = give(0, n, 0)
    wait(dec_copies)
    code_grad = join_halves(dot_nt(e[...], dec2[...]), left)
    grad = (code_grad * sig * (1.0 + pre * (1.0 - sig))).astype(BF).astype(F32)
    grads = split_halves(grad, left)
    bias = jnp.sum(grads[:, :n], axis=0, keepdims=True)
    wait(x_copies)
    fill(grads, x, n)
    for g in range(groups):
        shifted = pltpu.roll(bias, (n - g * (n // groups)) % n, 1)
        pieces[g, 2 * n :, :] = jnp.zeros((16, quarter), BF)
        pieces[g, 2 * n :, :n] = hi_lo(shifted)
    given += give(n, 2 * n + 16, 1)
    wait(given)


def hand_out(pieces, outs, me, sems):
    wait(start([(pieces.at[lax.rem(me + k, SIDE)], out) for k, out in enumerate(outs)], sems))


def gradients(x, err, pre_a, pre_b, dec):
    n, width = dec.shape
    piece = (2 * n + 16, width // SIDE)
    rows = 2 * pre_a.shape[0]
    in_vmem = pl.BlockSpec(memory_space=pltpu.VMEM)
    return pl.pallas_call(
        grad_kernel,
        in_specs=[in_vmem, in_vmem] + [ANY] * (2 * SIDE + 3),
        out_shape=[jax.ShapeDtypeStruct(piece, BF)] * SIDE,
        out_specs=[ANY] * SIDE,
        scratch_shapes=[
            pltpu.VMEM((2 * n, width // 2), BF),
            pltpu.VMEM((rows, width // 2), BF),
            pltpu.VMEM((rows, width // 2), BF),
            pltpu.VMEM((SIDE,) + piece, BF),
            pltpu.SemaphoreType.DMA((2,)),
            pltpu.SemaphoreType.DMA((SIDE + 1,)),
            pltpu.SemaphoreType.DMA((SIDE + 1,)),
            pltpu.SemaphoreType.DMA((2 * SIDE,)),
        ],
        compiler_params=PARAMS,
        name="gradients",
    )(pre_a, pre_b, dec, *x, *err)


def first_sum_kernel(*refs):
    ins, outs, (pieces, sems) = refs[:SIDE], refs[SIDE : 2 * SIDE], refs[2 * SIDE :]
    rows, quarter = ins[0].shape
    n = (rows - 16) // 2
    piece = pieces.shape[1] - 16
    total = ins[0][: 2 * n, :].astype(F32)
    bias = ins[0][2 * n :, :n].astype(F32)
    for part in ins[1:]:
        total = total + part[: 2 * n, :].astype(F32)
        bias = bias + part[2 * n :, :n].astype(F32)
    turned = total.T.astype(BF)
    bias = jnp.sum(bias, axis=0, keepdims=True)
    for c in range(SIDE):
        pieces[c, :piece, :] = turned[c * piece : (c + 1) * piece]
        shifted = pltpu.roll(bias, (n - c * (n // (SIDE * SIDE))) % n, 1)
        pieces[c, piece:, :n] = hi_lo(shifted)
        pieces[c, piece:, n:] = jnp.zeros((16, n), BF)
    hand_out(pieces, outs, lax.rem(lax.axis_index("rows"), SIDE), sems)


def first_sum(parts):
    rows, quarter = parts[0].shape
    piece = (quarter // SIDE + 16, rows - 16)
    return pl.pallas_call(
        first_sum_kernel,
        out_shape=[jax.ShapeDtypeStruct(piece, BF)] * SIDE,
        out_specs=[pl.BlockSpec(memory_space=pl.ANY)] * SIDE,
        scratch_shapes=[pltpu.VMEM((SIDE,) + piece, BF), pltpu.SemaphoreType.DMA((SIDE,))],
        compiler_params=PARAMS,
        name="sum_over_y",
    )(*parts)


def last_sum_kernel(*refs):
    ins, (enc_ref, dec_ref, bias_ref) = refs[:SIDE], refs[SIDE:]
    rows, cols = ins[0].shape
    piece, n = rows - 16, cols // 2
    total = ins[0][...].astype(F32)
    for part in ins[1:]:
        total = total + part[...].astype(F32)
    dec_ref[...] = total[:piece, :n]
    enc_ref[...] = total[:piece, n:]
    bias = jnp.sum(total[piece:, :n], axis=0, keepdims=True)
    bias_ref[...] = bias[:, : bias_ref.shape[1]]


def last_sum(parts, own):
    rows, cols = parts[0].shape
    piece, n = rows - 16, cols // 2
    return pl.pallas_call(
        last_sum_kernel,
        out_shape=[
            jax.ShapeDtypeStruct((piece, n), F32),
            jax.ShapeDtypeStruct((piece, n), F32),
            jax.ShapeDtypeStruct((1, own), F32),
        ],
        compiler_params=PARAMS,
        name="sum_over_z",
    )(*parts)


def share_pieces(pieces, along_y):
    got = [pieces[0]]
    for k in (2, 1, 3):
        pairs = []
        for i in range(SIDE * SIDE):
            y, z = divmod(i, SIDE)
            to = ((y + k) % SIDE, z) if along_y else (y, (z + k) % SIDE)
            pairs.append((i, to[0] * SIDE + to[1]))
        got.append(lax.ppermute(pieces[k], "rows", pairs))
    return got


def along_z(arrays, back=False):
    moved = {k: shift_z(arrays[k], STEPS[k], back) for k in (2, 1, 3)}
    return [arrays[0], moved[1], moved[2], moved[3]]


def shift_z(x, steps, back):
    pairs = []
    for i in range(512):
        rows, lat = divmod(i, 32)
        y, z_hi = divmod(rows, SIDE)
        x_place, rest = divmod(lat, 2 * SIDE)
        z_lo, core = divmod(rest, 2)
        step = -steps[core] if back else steps[core]
        z = (z_hi * SIDE + z_lo + step) % (SIDE * SIDE)
        to_rows = y * SIDE + z // SIDE
        pairs.append((i, to_rows * 32 + x_place * 2 * SIDE + z % SIDE * 2 + core))
    return lax.ppermute(x, ("rows", "lat"), pairs)


def over_x(x):
    groups = [
        [xp * 2 * SIDE + z * 2 + core for xp in range(SIDE) for core in range(2)]
        for z in range(SIDE)
    ]
    members = 2 * SIDE
    shape = x.shape
    out = lax.all_to_all(
        x.reshape(members, shape[0] // members, shape[1]),
        "lat",
        split_axis=0,
        concat_axis=0,
        axis_index_groups=groups,
        tiled=True,
    )
    return out.reshape(shape)


def to_owners(slots):
    moved = along_z(slots[:SIDE])
    merged, pieces = turn_pieces(moved, over_x(slots[SIDE]))
    stream_a = over_x(merged)
    stream_b = along_z(pieces)
    return stream_a, stream_b


def to_homes(stream_a, stream_b):
    moved = along_z(stream_b, True)
    merged, pieces = turn_pieces(moved, over_x(stream_a))
    home_b = over_x(merged)
    home_a = along_z(pieces, True)
    return [*home_a, home_b]


def local(activations, block_ids, enc_weight, enc_bias, dec_weight, dec_bias):
    blocks = lax.axis_size("lat")
    parts_rows = lax.axis_size("rows")
    n = enc_weight.shape[1]
    ids = block_ids.T
    bias = enc_bias[None, :]
    x_a, x_b = to_owners(pack(ids, activations, blocks))
    dec_a, pre_a = encode_decode([x_a], enc_weight, bias, dec_weight)
    x_b, dec_a = lax.optimization_barrier((x_b, dec_a))
    *dec_b, pre_b = encode_decode(x_b, enc_weight, bias, dec_weight)
    back = to_homes(dec_a, dec_b)
    e_a, e_b = to_owners(error_rows(ids, back, activations, dec_bias[None, :], blocks))
    terms = gradients([*x_b, x_a], [*e_b, e_a], pre_a, pre_b, dec_weight)
    terms = share_pieces(terms, True)
    terms = share_pieces(first_sum(terms), False)
    enc_grad, dec_turned, bias_grad = last_sum(terms, n // parts_rows)
    return enc_grad, dec_turned.T, bias_grad.reshape(-1)


def solution(mesh):
    in_specs = (
        P(("rows", "lat"), None),
        P(("rows", "lat"), None),
        P(None, "lat"),
        P("lat"),
        P("lat", None),
        P(),
    )
    out_specs = (P("rows", "lat"), P("lat", "rows"), P(("lat", "rows")))
    return jax.shard_map(local, mesh=mesh, in_specs=in_specs, out_specs=out_specs, check_vma=False)
```

```python
import functools

import jax
import jax.numpy as jnp
from jax import lax
from jax.experimental import pallas as pl
from jax.experimental.pallas import tpu as pltpu
from jax.sharding import PartitionSpec as P

SLOTS = 6
PAIR = 2 * SLOTS
SIDE = 4
STEPS = ((0, 0), (2, -2), (1, 1), (-1, -1))
BF = jnp.bfloat16
F32 = jnp.float32
VMEM = 56 * 1024 * 1024
COLS = 256
PARAMS = pltpu.CompilerParams(vmem_limit_bytes=VMEM)
ANY = pl.BlockSpec(memory_space=pl.ANY)


def by_twelve(row):
    return lax.shift_right_logical(row * 5462, 16)


def dot(a, b):
    return lax.dot_general(a, b, (((1,), (0,)), ((), ())), preferred_element_type=F32)


def dot_nt(a, b):
    return lax.dot_general(a, b, (((1,), (1,)), ((), ())), preferred_element_type=F32)


def left_rows(rows):
    row = lax.broadcasted_iota(jnp.int32, (rows, 1), 0)
    return row - by_twelve(row) * PAIR < SLOTS


def split_halves(x, left):
    zero = jnp.zeros_like(x)
    return jnp.concatenate([jnp.where(left, x, zero), jnp.where(left, zero, x)], axis=1)


def join_halves(y, left):
    rows, n = y.shape[0], y.shape[1] // 2
    yl, yr = y[:, :n], y[:, n:]
    after = pltpu.roll(yr, rows - SLOTS, 0)
    before = pltpu.roll(yl, SLOTS, 0)
    return jnp.where(left, yl + after, yr + before)


def one_hot_slots(ids, blocks):
    n = ids.shape[1]
    rows = 2 * blocks * PAIR
    number = lax.broadcasted_iota(jnp.int32, (blocks, n), 0)
    member = (number == ids[0:1, :]) | (number == ids[1:2, :])
    earlier = (
        lax.broadcasted_iota(jnp.int32, (n, n), 0) < lax.broadcasted_iota(jnp.int32, (n, n), 1)
    )
    position = dot(member.astype(F32).astype(BF), earlier.astype(F32).astype(BF))
    code = jnp.where(member, position, 200.0).astype(BF)
    zl = lax.rem(lax.axis_index("lat") // 2, SIDE)
    row = lax.broadcasted_iota(jnp.int32, (rows, 1), 0)
    piece = by_twelve(row)
    place = row - piece * PAIR
    first = piece < blocks
    in_a, in_b = piece, piece - blocks
    xc = jnp.where(first, in_a & 7, lax.shift_right_logical(in_b, 2))
    k = jnp.where(first, lax.shift_right_logical(in_a, 3), in_b & 3)
    up = jnp.where((k == 1) | (k == 2), 3 - k, k)
    block = lax.shift_right_logical(xc, 1) * (2 * SIDE) + ((zl + up) & 3) * 2 + (xc & 1)
    left = place < SLOTS
    slot = place - jnp.where(left, 0, SLOTS) + jnp.where(first, 0, SLOTS)
    expand = lax.broadcasted_iota(jnp.int32, (rows, blocks), 1) == block
    spread = dot(expand.astype(F32).astype(BF), code)
    hit = (spread == slot.astype(F32)).astype(F32)
    return split_halves(hit, left)


def start(pairs, sems, first=0):
    copies = [pltpu.make_async_copy(a, b, sems.at[first + i]) for i, (a, b) in enumerate(pairs)]
    for copy in copies:
        copy.start()
    return copies


def wait(copies):
    for copy in copies:
        copy.wait()


def send_slots(sel, rows2, slots, outs, sems):
    total, half = slots.shape
    rows = total // 2
    part = rows // SIDE
    copies = []
    for i in range(2):
        own = slice(i * rows, (i + 1) * rows)
        chosen = sel[own, :]
        for c in range(0, half, COLS):
            slots[own, c : c + COLS] = dot(chosen, rows2[:, c : c + COLS]).astype(BF)
        if i == 0:
            copies += start(
                [(slots.at[k * part : (k + 1) * part], outs[k]) for k in range(SIDE)], sems
            )
        else:
            copies += start([(slots.at[rows:], outs[SIDE])], sems, SIDE)
    wait(copies)


def slot_shapes(blocks, half):
    total = blocks * PAIR
    part = total // SIDE
    shapes = [jax.ShapeDtypeStruct((part, half), BF)] * SIDE
    return shapes + [jax.ShapeDtypeStruct((total, half), BF)]


def pack_kernel(blocks, ids_ref, act_ref, *refs):
    outs, (act2, sel, pieces, in_sems, sems) = refs[: SIDE + 1], refs[SIDE + 1 :]
    n, width = act_ref.shape
    half = width // 2
    copies = start(
        [(act_ref.at[:, s * half : (s + 1) * half], act2.at[s * n : (s + 1) * n]) for s in range(2)],
        in_sems,
    )
    sel[...] = one_hot_slots(ids_ref[...], blocks).astype(BF)
    wait(copies)
    send_slots(sel, act2, pieces, outs, sems)


def pack(ids, act, blocks):
    n, width = act.shape
    half = width // 2
    part = blocks * PAIR // SIDE
    return pl.pallas_call(
        functools.partial(pack_kernel, blocks),
        in_specs=[pl.BlockSpec(memory_space=pltpu.VMEM), ANY],
        out_specs=[ANY] * (SIDE + 1),
        out_shape=slot_shapes(blocks, half),
        scratch_shapes=[
            pltpu.VMEM((2 * n, half), BF),
            pltpu.VMEM((2 * SIDE * part, 2 * n), BF),
            pltpu.VMEM((2 * SIDE * part, half), BF),
            pltpu.SemaphoreType.DMA((2,)),
            pltpu.SemaphoreType.DMA((SIDE + 1,)),
        ],
        compiler_params=PARAMS,
        name="pack_rows",
    )(ids, act)


def swap_kernel(merge, *refs):
    if merge:
        ins, out_ref, (pieces, done, in_sems, sems) = refs[:SIDE], refs[SIDE], refs[SIDE + 1 :]
    else:
        in_ref, outs, (pieces, done, in_sems, sems) = refs[0], refs[1 : SIDE + 1], refs[SIDE + 1 :]
    rows = pieces.shape[1]
    part = rows // SIDE
    halves = range(2)
    if merge:
        moves = [
            [
                (ins[k].at[h * part : (h + 1) * part], pieces.at[h, k * part : (k + 1) * part])
                for k in range(SIDE)
            ]
            for h in halves
        ]
    else:
        moves = [[(in_ref.at[h * rows : (h + 1) * rows], pieces.at[h])] for h in halves]
    copies = [start(moves[h], in_sems, h * SIDE) for h in halves]
    row = lax.broadcasted_iota(jnp.int32, (rows, 1), 0)
    piece = by_twelve(row)
    source = (piece & 3) * part + lax.shift_right_logical(piece, 2) * PAIR + row - piece * PAIR
    turn = (lax.broadcasted_iota(jnp.int32, (rows, rows), 1) == source).astype(F32).astype(BF)
    sent = []
    for h in halves:
        wait(copies[h])
        done[h] = dot(turn, pieces[h]).astype(BF)
        if merge:
            sent += start([(done.at[h], out_ref.at[h * rows : (h + 1) * rows])], sems, h * SIDE)
        else:
            sent += start(
                [
                    (done.at[h, k * part : (k + 1) * part], outs[k].at[h * part : (h + 1) * part])
                    for k in range(SIDE)
                ],
                sems,
                h * SIDE,
            )
    wait(sent)


def swap_pieces(arrays, merge):
    total = arrays[0].shape[0] * (SIDE if merge else 1)
    half = arrays[0].shape[1]
    shape = jax.ShapeDtypeStruct((total, half), BF)
    shapes = [jax.ShapeDtypeStruct((total // SIDE, half), BF)] * SIDE
    return pl.pallas_call(
        functools.partial(swap_kernel, merge),
        in_specs=[ANY] * len(arrays),
        out_specs=ANY if merge else [ANY] * SIDE,
        out_shape=shape if merge else shapes,
        scratch_shapes=[
            pltpu.VMEM((2, total // 2, half), BF),
            pltpu.VMEM((2, total // 2, half), BF),
            pltpu.SemaphoreType.DMA((2 * SIDE,)),
            pltpu.SemaphoreType.DMA((2 * SIDE,)),
        ],
        compiler_params=PARAMS,
        name="merge_pieces" if merge else "split_pieces",
    )(*arrays)


def code_kernel(parts, *refs):
    ins, (enc_ref, bias_ref, dec_ref) = refs[:parts], refs[parts : parts + 3]
    outs, pre_ref = refs[parts + 3 : 2 * parts + 3], refs[2 * parts + 3]
    enc2, dec2, x, done, w_sems, in_sems, sems = refs[2 * parts + 4 :]
    half, n = enc2.shape[0], enc2.shape[1] // 2
    total = x.shape[0]
    rows = total // parts

    def moves(refs, buffer):
        return [(refs[i], buffer.at[i * rows : (i + 1) * rows]) for i in range(parts)]

    enc_copies = start(
        [(enc_ref.at[s * half : (s + 1) * half], enc2.at[:, s * n : (s + 1) * n]) for s in range(2)],
        w_sems,
    )
    in_copies = start(moves(ins, x), in_sems)
    dec_copies = start(
        [(dec_ref.at[:, s * half : (s + 1) * half], dec2.at[s * n : (s + 1) * n]) for s in range(2)],
        w_sems,
        2,
    )
    left = left_rows(total)
    wait(enc_copies)
    wait(in_copies)
    pre = join_halves(dot(x[...], enc2[...]), left) + bias_ref[...]
    pre_ref[...] = pre
    codes = split_halves(pre * jax.nn.sigmoid(pre), left).astype(BF)
    wait(dec_copies)
    for c in range(0, half, COLS):
        done[:, c : c + COLS] = dot(codes, dec2[:, c : c + COLS]).astype(BF)
    wait(start([(b, a) for a, b in moves(outs, done)], sems))


def encode_decode(x, enc, bias, dec):
    width, n = enc.shape
    half = width // 2
    parts = len(x)
    total = sum(a.shape[0] for a in x)
    return pl.pallas_call(
        functools.partial(code_kernel, parts),
        in_specs=[ANY] * (parts + 1) + [pl.BlockSpec(memory_space=pltpu.VMEM), ANY],
        out_specs=[ANY] * parts + [pl.BlockSpec(memory_space=pltpu.VMEM)],
        out_shape=[jax.ShapeDtypeStruct(a.shape, BF) for a in x]
        + [jax.ShapeDtypeStruct((total, n), F32)],
        scratch_shapes=[
            pltpu.VMEM((half, 2 * n), BF),
            pltpu.VMEM((2 * n, half), BF),
            pltpu.VMEM((total, half), BF),
            pltpu.VMEM((total, half), BF),
            pltpu.SemaphoreType.DMA((4,)),
            pltpu.SemaphoreType.DMA((SIDE,)),
            pltpu.SemaphoreType.DMA((SIDE,)),
        ],
        compiler_params=pltpu.CompilerParams(vmem_limit_bytes=16 * 1024 * 1024),
        name="encode_decode",
    )(*x, enc, bias, dec)


def slot_moves(refs, buffer):
    part = refs[0].shape[0]
    pairs = [(refs[k], buffer.at[k * part : (k + 1) * part]) for k in range(SIDE)]
    return pairs + [(refs[SIDE], buffer.at[SIDE * part :])]


def error_kernel(blocks, ids_ref, bias_ref, act_ref, *refs):
    ins, outs = refs[: SIDE + 1], refs[SIDE + 1 : 2 * SIDE + 2]
    act2, back, sel, err2, pieces, act_sems, in_sems, sems = refs[2 * SIDE + 2 :]
    n, width = act_ref.shape
    half = width // 2
    copies = start(slot_moves(ins, back), in_sems)
    copies += start(
        [(act_ref.at[:, s * half : (s + 1) * half], act2.at[s * n : (s + 1) * n]) for s in range(2)],
        act_sems,
    )
    hits = one_hot_slots(ids_ref[...], blocks)
    sel[...] = hits.astype(BF)
    turned = hits.T.astype(BF)
    wait(copies)
    step = COLS
    for c in range(0, half, step):
        sums = dot(turned, back[:, c : c + step])
        for s in range(2):
            rows = slice(s * n, (s + 1) * n)
            bias = bias_ref[:, s * half + c : s * half + c + step]
            wanted = act2[rows, c : c + step].astype(F32)
            err2[rows, c : c + step] = ((sums[rows] + bias - wanted) * (1.0 / 64.0)).astype(BF)
    send_slots(sel, err2, pieces, outs, sems)


def error_rows(ids, back, act, bias, blocks):
    n, width = act.shape
    half = width // 2
    total = 2 * blocks * PAIR
    in_vmem = pl.BlockSpec(memory_space=pltpu.VMEM)
    return pl.pallas_call(
        functools.partial(error_kernel, blocks),
        in_specs=[in_vmem, in_vmem] + [ANY] * (SIDE + 2),
        out_specs=[ANY] * (SIDE + 1),
        out_shape=slot_shapes(blocks, half),
        scratch_shapes=[
            pltpu.VMEM((2 * n, half), BF),
            pltpu.VMEM((total, half), BF),
            pltpu.VMEM((total, 2 * n), BF),
            pltpu.VMEM((2 * n, half), BF),
            pltpu.VMEM((total, half), BF),
            pltpu.SemaphoreType.DMA((2,)),
            pltpu.SemaphoreType.DMA((SIDE + 1,)),
            pltpu.SemaphoreType.DMA((SIDE + 1,)),
        ],
        compiler_params=PARAMS,
        name="error_rows",
    )(ids, bias, act, *back)


def hi_lo(x):
    hi = x.astype(BF).astype(F32)
    row = lax.broadcasted_iota(jnp.int32, (16, x.shape[1]), 0)
    return jnp.where(row == 0, hi, jnp.where(row == 1, x - hi, 0.0)).astype(BF)


def grad_kernel(pre_a, pre_b, dec_ref, *refs):
    x_refs, e_refs, outs = refs[: SIDE + 1], refs[SIDE + 1 : 2 * SIDE + 2], refs[2 * SIDE + 2 : 3 * SIDE + 2]
    dec2, x, e, pieces, w_sems, x_sems, e_sems, sems = refs[3 * SIDE + 2 :]
    rows, half = x.shape
    n = pre_a.shape[1]
    groups, _, quarter = pieces.shape
    e_copies = start(slot_moves(e_refs, e), e_sems)
    dec_copies = start(
        [(dec_ref.at[:, s * half : (s + 1) * half], dec2.at[s * n : (s + 1) * n]) for s in range(2)],
        w_sems,
    )
    x_copies = start(slot_moves(x_refs, x), x_sems)
    me = lax.axis_index("rows") // SIDE
    left = left_rows(rows)
    pre = jnp.concatenate([pre_b[...], pre_a[...]], axis=0)
    sig = jax.nn.sigmoid(pre)
    codes = split_halves((pre * sig).astype(BF).astype(F32), left)

    def fill(terms, slots, first):
        turned = terms.T.astype(BF)
        for g in range(groups // 2):
            both = dot(turned, slots[:, g * quarter : (g + 1) * quarter]).astype(BF)
            for s in range(2):
                pieces[g + s * (groups // 2), first : first + n, :] = both[s * n : (s + 1) * n]

    def give(first, last, turn):
        return start(
            [
                (pieces.at[lax.rem(me + k, SIDE), first:last], out.at[first:last])
                for k, out in enumerate(outs)
            ],
            sems,
            turn * SIDE,
        )

    wait(e_copies)
    fill(codes, e, 0)
    given = give(0, n, 0)
    wait(dec_copies)
    code_grad = join_halves(dot_nt(e[...], dec2[...]), left)
    grad = (code_grad * sig * (1.0 + pre * (1.0 - sig))).astype(BF).astype(F32)
    grads = split_halves(grad, left)
    bias = jnp.sum(grads[:, :n], axis=0, keepdims=True)
    wait(x_copies)
    fill(grads, x, n)
    for g in range(groups):
        shifted = pltpu.roll(bias, (n - g * (n // groups)) % n, 1)
        pieces[g, 2 * n :, :] = jnp.zeros((16, quarter), BF)
        pieces[g, 2 * n :, :n] = hi_lo(shifted)
    given += give(n, 2 * n + 16, 1)
    wait(given)


def hand_out(pieces, outs, me, sems):
    wait(start([(pieces.at[lax.rem(me + k, SIDE)], out) for k, out in enumerate(outs)], sems))


def gradients(x, err, pre_a, pre_b, dec):
    n, width = dec.shape
    piece = (2 * n + 16, width // SIDE)
    rows = 2 * pre_a.shape[0]
    in_vmem = pl.BlockSpec(memory_space=pltpu.VMEM)
    return pl.pallas_call(
        grad_kernel,
        in_specs=[in_vmem, in_vmem] + [ANY] * (2 * SIDE + 3),
        out_shape=[jax.ShapeDtypeStruct(piece, BF)] * SIDE,
        out_specs=[ANY] * SIDE,
        scratch_shapes=[
            pltpu.VMEM((2 * n, width // 2), BF),
            pltpu.VMEM((rows, width // 2), BF),
            pltpu.VMEM((rows, width // 2), BF),
            pltpu.VMEM((SIDE,) + piece, BF),
            pltpu.SemaphoreType.DMA((2,)),
            pltpu.SemaphoreType.DMA((SIDE + 1,)),
            pltpu.SemaphoreType.DMA((SIDE + 1,)),
            pltpu.SemaphoreType.DMA((2 * SIDE,)),
        ],
        compiler_params=PARAMS,
        name="gradients",
    )(pre_a, pre_b, dec, *x, *err)


def first_sum_kernel(*refs):
    ins, outs, (pieces, sems) = refs[:SIDE], refs[SIDE : 2 * SIDE], refs[2 * SIDE :]
    rows, quarter = ins[0].shape
    n = (rows - 16) // 2
    piece = pieces.shape[1] - 16
    total = ins[0][: 2 * n, :].astype(F32)
    bias = ins[0][2 * n :, :n].astype(F32)
    for part in ins[1:]:
        total = total + part[: 2 * n, :].astype(F32)
        bias = bias + part[2 * n :, :n].astype(F32)
    turned = total.T.astype(BF)
    bias = jnp.sum(bias, axis=0, keepdims=True)
    for c in range(SIDE):
        pieces[c, :piece, :] = turned[c * piece : (c + 1) * piece]
        shifted = pltpu.roll(bias, (n - c * (n // (SIDE * SIDE))) % n, 1)
        pieces[c, piece:, :n] = hi_lo(shifted)
        pieces[c, piece:, n:] = jnp.zeros((16, n), BF)
    hand_out(pieces, outs, lax.rem(lax.axis_index("rows"), SIDE), sems)


def first_sum(parts):
    rows, quarter = parts[0].shape
    piece = (quarter // SIDE + 16, rows - 16)
    return pl.pallas_call(
        first_sum_kernel,
        out_shape=[jax.ShapeDtypeStruct(piece, BF)] * SIDE,
        out_specs=[pl.BlockSpec(memory_space=pl.ANY)] * SIDE,
        scratch_shapes=[pltpu.VMEM((SIDE,) + piece, BF), pltpu.SemaphoreType.DMA((SIDE,))],
        compiler_params=PARAMS,
        name="sum_over_y",
    )(*parts)


def last_sum_kernel(*refs):
    ins, (enc_ref, dec_ref, bias_ref) = refs[:SIDE], refs[SIDE:]
    rows, cols = ins[0].shape
    piece, n = rows - 16, cols // 2
    total = ins[0][...].astype(F32)
    for part in ins[1:]:
        total = total + part[...].astype(F32)
    dec_ref[...] = total[:piece, :n]
    enc_ref[...] = total[:piece, n:]
    bias = jnp.sum(total[piece:, :n], axis=0, keepdims=True)
    bias_ref[...] = bias[:, : bias_ref.shape[1]]


def last_sum(parts, own):
    rows, cols = parts[0].shape
    piece, n = rows - 16, cols // 2
    return pl.pallas_call(
        last_sum_kernel,
        out_shape=[
            jax.ShapeDtypeStruct((piece, n), F32),
            jax.ShapeDtypeStruct((piece, n), F32),
            jax.ShapeDtypeStruct((1, own), F32),
        ],
        compiler_params=PARAMS,
        name="sum_over_z",
    )(*parts)


def share_pieces(pieces, along_y):
    got = [pieces[0]]
    for k in (2, 1, 3):
        pairs = []
        for i in range(SIDE * SIDE):
            y, z = divmod(i, SIDE)
            to = ((y + k) % SIDE, z) if along_y else (y, (z + k) % SIDE)
            pairs.append((i, to[0] * SIDE + to[1]))
        got.append(lax.ppermute(pieces[k], "rows", pairs))
    return got


def along_z(arrays, back=False):
    return [arrays[0]] + [shift_z(arrays[k], STEPS[k], back) for k in range(1, SIDE)]


def shift_z(x, steps, back):
    pairs = []
    for i in range(512):
        rows, lat = divmod(i, 32)
        y, z_hi = divmod(rows, SIDE)
        x_place, rest = divmod(lat, 2 * SIDE)
        z_lo, core = divmod(rest, 2)
        step = -steps[core] if back else steps[core]
        z = (z_hi * SIDE + z_lo + step) % (SIDE * SIDE)
        to_rows = y * SIDE + z // SIDE
        pairs.append((i, to_rows * 32 + x_place * 2 * SIDE + z % SIDE * 2 + core))
    return lax.ppermute(x, ("rows", "lat"), pairs)


def over_x(x):
    groups = [
        [xp * 2 * SIDE + z * 2 + core for xp in range(SIDE) for core in range(2)]
        for z in range(SIDE)
    ]
    members = 2 * SIDE
    shape = x.shape
    out = lax.all_to_all(
        x.reshape(members, shape[0] // members, shape[1]),
        "lat",
        split_axis=0,
        concat_axis=0,
        axis_index_groups=groups,
        tiled=True,
    )
    return out.reshape(shape)


def to_owners(slots):
    moved = along_z(slots[:SIDE])
    pieces = swap_pieces([over_x(slots[SIDE])], False)
    pieces, moved = lax.optimization_barrier((pieces, moved))
    stream_a = over_x(swap_pieces(moved, True))
    stream_b = along_z(pieces)
    return stream_a, stream_b


def to_homes(stream_a, stream_b):
    moved = along_z(stream_b, True)
    pieces = swap_pieces([over_x(stream_a)], False)
    pieces, moved = lax.optimization_barrier((pieces, moved))
    home_b = over_x(swap_pieces(moved, True))
    home_a = along_z(pieces, True)
    return [*home_a, home_b]


def local(activations, block_ids, enc_weight, enc_bias, dec_weight, dec_bias):
    blocks = lax.axis_size("lat")
    parts_rows = lax.axis_size("rows")
    n = enc_weight.shape[1]
    ids = block_ids.T
    bias = enc_bias[None, :]
    x_a, x_b = to_owners(pack(ids, activations, blocks))
    dec_a, pre_a = encode_decode([x_a], enc_weight, bias, dec_weight)
    x_b, dec_a = lax.optimization_barrier((x_b, dec_a))
    *dec_b, pre_b = encode_decode(x_b, enc_weight, bias, dec_weight)
    back = to_homes(dec_a, dec_b)
    e_a, e_b = to_owners(error_rows(ids, back, activations, dec_bias[None, :], blocks))
    terms = gradients([*x_b, x_a], [*e_b, e_a], pre_a, pre_b, dec_weight)
    terms = share_pieces(terms, True)
    terms = share_pieces(first_sum(terms), False)
    enc_grad, dec_turned, bias_grad = last_sum(terms, n // parts_rows)
    return enc_grad, dec_turned.T, bias_grad.reshape(-1)


def solution(mesh):
    in_specs = (
        P(("rows", "lat"), None),
        P(("rows", "lat"), None),
        P(None, "lat"),
        P("lat"),
        P("lat", None),
        P(),
    )
    out_specs = (P("rows", "lat"), P("lat", "rows"), P(("lat", "rows")))
    return jax.shard_map(local, mesh=mesh, in_specs=in_specs, out_specs=out_specs, check_vma=False)
```
